512 devices in a mesh: row: 16 (over z_hi, x), col: 32 (over z_lo, y, core).
Axes of the slice: x: 4, y: 8, z: 8 (z_hi: 4, z_lo: 2; z = z_hi * 2 + z_lo), core: 2. Of those that a mesh axis runs over, the one named last changes fastest.
Arguments:
- pair: bfloat16 [768, 768, 128], P('row', 'col'), may hold values from -6 to 6
- pair_mask: int32 [768, 768], P('row', 'col'), may hold values 0 or 1
- in_gain: float32 [128], replicated, may hold values from 0.1 to 1.9
- in_bias: float32 [128], replicated, may hold values from -2.5 to 2.5
- proj_weight: bfloat16 [128, 512], replicated, may hold values from -0.5 to 0.5
- gate_weight: bfloat16 [128, 128], replicated, may hold values from -0.5 to 0.5
- out_gain: float32 [128], replicated, may hold values from 0.1 to 1.9
- out_bias: float32 [128], replicated, may hold values from -2.5 to 2.5
- out_weight: bfloat16 [128, 128], replicated, may hold values from -0.5 to 0.5
Outputs:
- update: bfloat16 [768, 768, 128], P('row', 'col')
The draws below stay inside these ranges and needn't reach their ends.
All inputs are finite; a program needn't handle non-finite values. No bound on the sum of `pair_mask` on one device may be relied on, other than what follows from the above.
Results may differ from the reference program's by a relative error of at most 0.0052.
Values may be sent and summed in bfloat16 or wider, within the bound.
No kernel may reach another device: no remote copies, remote signals or barrier semaphores. Data moves between devices by JAX's collectives and lax.ppermute only.
A program may use at most 128 MiB of HBM per device.

```python
import jax
import jax.numpy as jnp
from jax import lax

C = 128
N = 768


def touch_ends(entries, key, least, high):
    index_at = [jax.random.randint(jax.random.fold_in(key, axis), (), 0, length) for axis, length in enumerate(entries.shape)]
    widest = entries.shape.index(max(entries.shape))
    beside = index_at[:widest] + [(index_at[widest] + 1) % entries.shape[widest]] + index_at[widest + 1:]
    return entries.at[tuple(index_at)].set(least).at[tuple(beside)].set(high)


def levels(rng, extent, cuts, smallest, high):
    def one(position, shards_of):
        steps = jax.random.uniform(jax.random.fold_in(jax.random.fold_in(rng, 6), position), (shards_of,), jnp.float32, smallest / len(cuts), high / len(cuts))
        return jnp.repeat(jnp.exp(steps), extent[position] // shards_of).reshape((-1,) + (1,) * (len(extent) - position - 1))

    level = one(*cuts[0])
    for cut in cuts[1:]:
        level = level * one(*cut)
    return level


def scatter_about(rng, extent, deviation, limit, shards=(), held_as=jnp.bfloat16):
    entries = jax.random.normal(rng, extent, jnp.float32) * deviation
    if len(shards) > 0:
        entries = levels(rng, extent, shards, -0.22, 0.18) * entries
    return jnp.clip(entries, min=-limit, max=limit).astype(held_as)


def setup_inputs(seed: int = 0) -> dict:
    splits = jax.random.split(jax.random.key(seed), 10)
    return {
        "pair": scatter_about(splits[0], (N, N, C), 1.0, 6.0, ((0, 16), (1, 32))),
        "pair_mask": touch_ends((jax.random.randint(splits[1], (N, N), 0, 8) < 7).astype(jnp.int32), jax.random.fold_in(splits[1], 1), 0, 1),
        "in_gain": jnp.clip(1.0 + 0.18 * jax.random.normal(splits[2], (C,), jnp.float32), 0.1, 1.9),
        "in_bias": scatter_about(splits[3], (C,), 0.5, 2.5, (), jnp.float32),
        "proj_weight": scatter_about(splits[4], (C, 4 * C), C ** -0.5, 0.5),
        "gate_weight": scatter_about(splits[5], (C, C), C ** -0.5, 0.5),
        "out_gain": jnp.clip(1.0 + 0.18 * jax.random.normal(splits[6], (C,), jnp.float32), 0.1, 1.9),
        "out_bias": scatter_about(splits[7], (C,), 0.5, 2.5, (), jnp.float32),
        "out_weight": scatter_about(splits[8], (C, C), C ** -0.5, 0.5),
    }


def layer_norm(values, gain, bias):
    values = values.astype(jnp.float32)
    mean = lax.optimization_barrier(jnp.mean(values, axis=-1, keepdims=True))
    centred = values - mean
    var = lax.optimization_barrier(jnp.mean(centred * centred, axis=-1, keepdims=True))
    return centred * lax.rsqrt(var + 1e-05) * gain + bias

def factor(normed, weight, mask_values):
    width = normed.shape[-1]
    flat = normed.reshape(-1, width)
    hidden = jnp.dot(flat, weight, preferred_element_type=jnp.float32)
    hidden = hidden.reshape(normed.shape[:-1] + (2 * width,))
    result = jax.nn.sigmoid(hidden[..., width:]) * hidden[..., :width]
    return (result * mask_values[..., None]).astype(jnp.bfloat16)

def reference(pair, pair_mask, in_gain, in_bias, proj_weight, gate_weight, out_gain, out_bias, out_weight):
    normed = layer_norm(pair, in_gain, in_bias).astype(jnp.bfloat16)
    mask_values = pair_mask.astype(jnp.float32)
    left = factor(normed, proj_weight[:, :2 * C], mask_values)
    right = factor(normed, proj_weight[:, 2 * C:], mask_values)
    gate = jax.nn.sigmoid(jnp.dot(normed.reshape(-1, C), gate_weight, preferred_element_type=jnp.float32))
    combined = jnp.einsum('ikc,jkc->ijc', left.astype(jnp.float32), right.astype(jnp.float32), precision=lax.Precision.HIGHEST)
    onorm = layer_norm(combined, out_gain, out_bias).astype(jnp.bfloat16)
    projected = jnp.dot(onorm.reshape(-1, C), out_weight, preferred_element_type=jnp.float32)
    return (gate * projected).reshape(N, N, C).astype(jnp.bfloat16)
```

```python
import functools

import jax
import jax.numpy as jnp
from jax import lax
from jax.experimental import pallas as pl
from jax.experimental.pallas import tpu as pltpu
from jax.sharding import PartitionSpec as P

BF16 = jnp.bfloat16
F32 = jnp.float32
AXES = ("row", "col")
ROWS, COLS, WIDTH = 48, 24, 128
HALF = COLS // 2
SPAN = HALF * ROWS
RPOS, QPOS = 8, 16
LANES = 128
SIDE = RPOS * ROWS
JSPAN = RPOS * COLS


def sigmoid(x):
    return 0.5 * jnp.tanh(0.5 * x) + 0.5


def device(z_hi, x, z_lo, y, core):
    return (z_hi * 4 + x) * 32 + z_lo * 16 + y * 2 + core


def x_of(side, x_low):
    return x_low if side == 0 else 3 - x_low


def positions():
    return [(zh, xl, zl, y) for zh in range(4) for xl in range(2) for zl in range(2) for y in range(8)]


def channel_groups():
    return [
        [device(zh, x_of(side, xl), zl, y, core) for zh, xl, zl, y in positions()]
        for side in range(2)
        for core in range(2)
    ]


def quad_groups():
    return [
        [device(zh, x_of(side, xl), zl, y, core) for side in range(2) for core in range(2)]
        for zh, xl, zl, y in positions()
    ]


def core_swap():
    return [(d, d ^ 1) for d in range(512)]


def dot(a, b, dims):
    return lax.dot_general(a, b, (dims, ((), ())), preferred_element_type=F32)


def call(kernel, out_shape, scratch=(), name=None):
    return pl.pallas_call(
        kernel,
        out_shape=out_shape,
        scratch_shapes=list(scratch),
        compiler_params=pltpu.CompilerParams(vmem_limit_bytes=16 * 2**20),
        name=name,
    )


def factors_kernel(x_ref, mask_ref, gain_ref, bias_ref, w_ref, send_ref, normed_ref, tokens, pairs):
    tokens[...] = x_ref[...].astype(F32)
    values = jnp.concatenate([tokens[pl.ds(k, ROWS, stride=COLS), :] for k in range(COLS)], axis=0)
    mean = jnp.mean(values, axis=-1, keepdims=True)
    centred = values - mean
    var = jnp.mean(centred * centred, axis=-1, keepdims=True)
    normed = (centred * lax.rsqrt(var + 1e-05) * gain_ref[...] + bias_ref[...]).astype(BF16)
    normed_ref[...] = normed
    token = lax.broadcasted_iota(jnp.int32, (ROWS, ROWS * COLS), 1)
    spread = (lax.rem(token, ROWS) == lax.broadcasted_iota(jnp.int32, token.shape, 0)).astype(BF16)
    every = dot(mask_ref[...].astype(F32).astype(BF16), spread, ((1,), (0,)))
    token = lax.broadcasted_iota(jnp.int32, every.shape, 1)
    first = lax.broadcasted_iota(jnp.int32, every.shape, 0) * ROWS
    mask = jnp.sum(jnp.where((token >= first) & (token < first + ROWS), every, 0.0), axis=0, keepdims=True)
    weight = w_ref[...].T
    for half in range(2):
        part = normed[half * SPAN : (half + 1) * SPAN]
        part_mask = mask[:, half * SPAN : (half + 1) * SPAN]
        sides = []
        for side in range(2):
            hidden = dot(weight[side * 2 * WIDTH : (side + 1) * 2 * WIDTH], part, ((1,), (1,)))
            sides.append(sigmoid(hidden[WIDTH:]) * hidden[:WIDTH] * part_mask)
        both = jnp.concatenate(sides, axis=1)
        for t in range(2 * SPAN // LANES):
            pairs[t, pl.ds(half, WIDTH, stride=2), :] = both[:, t * LANES : (t + 1) * LANES]
    for t in range(2 * SPAN // LANES):
        send_ref[:, :, t * LANES : (t + 1) * LANES] = pairs[t].astype(BF16).reshape(WIDTH, 2, LANES)


def gate_kernel(normed_ref, w_ref, gate_ref):
    gate_ref[...] = sigmoid(dot(normed_ref[...], w_ref[...], ((1,), (0,))))


def right_kernel(x_ref, out_ref):
    x = x_ref[...].reshape(RPOS * QPOS * 2, 2 * SPAN)[:, SPAN:]
    rows = 2 * QPOS
    for b in range(2):
        for k in range(HALF // 2):
            block = jnp.concatenate(
                [
                    x[rp * rows : (rp + 1) * rows, (h * 6 + k) * ROWS + b * COLS : (h * 6 + k) * ROWS + (b + 1) * COLS]
                    for h in range(2)
                    for rp in range(RPOS)
                ],
                axis=1,
            )
            out_ref[b, k * rows : (k + 1) * rows, :] = block
            out_ref[2 + b, k * rows : (k + 1) * rows, :] = block


def left_kernel(x_ref, out_ref):
    x = x_ref[...].reshape(RPOS * QPOS * 2, 2 * SPAN)[:, :SPAN]
    rows = 2 * QPOS
    for k in range(HALF):
        out_ref[k * rows : (k + 1) * rows, :] = jnp.concatenate(
            [x[rp * rows : (rp + 1) * rows, k * ROWS : (k + 1) * ROWS] for rp in range(RPOS)], axis=1
        )


def contract_kernel(own_ref, other_ref, right_ref, core_ref, send_ref, total):
    core = core_ref[0]
    own, other = own_ref[...], other_ref[...]
    left = [jnp.where(core == b, own, other) for b in range(2)]
    for side in range(2):
        part = jnp.zeros((JSPAN, SIDE), F32)
        for b in range(2):
            right = right_ref[side * 2 + b]
            for h in range(2):
                part += dot(right[:, h * JSPAN : (h + 1) * JSPAN], left[b][h * JSPAN : (h + 1) * JSPAN], ((0,), (0,)))
        for rp in range(RPOS):
            row = (rp // 2) * 4 + x_of(side, rp % 2)
            for t in range(SIDE // LANES):
                total[t, row * COLS : (row + 1) * COLS, :] = part[rp * COLS : (rp + 1) * COLS, t * LANES : (t + 1) * LANES]
    rows = 2 * QPOS
    blocks = [
        jnp.concatenate([total[t, pl.ds(j, rows, stride=HALF), :] for t in range(SIDE // LANES)], axis=1)
        for j in range(HALF)
    ]
    for rp in range(RPOS):
        piece = jnp.concatenate([block[:, rp * ROWS : (rp + 1) * ROWS] for block in blocks], axis=1)
        send_ref[rp * QPOS : (rp + 1) * QPOS] = piece.astype(BF16).reshape(QPOS, 2, SPAN)


def update_kernel(x_ref, gate_ref, gain_ref, bias_ref, w_ref, out_ref, pairs, tokens):
    arrived = x_ref[...].reshape(2 * WIDTH, SPAN).astype(F32)
    tiles = pl.cdiv(SPAN, LANES)
    for t in range(tiles):
        tile = arrived[:, t * LANES : (t + 1) * LANES]
        pairs[t, :, : tile.shape[1]] = tile
    for half in range(2):
        values = [pairs[t, pl.ds(half, WIDTH, stride=2), :] for t in range(tiles)]
        values = jnp.concatenate(values, axis=1)[:, :SPAN]
        mean = jnp.mean(values, axis=0, keepdims=True)
        centred = values - mean
        var = jnp.mean(centred * centred, axis=0, keepdims=True)
        onorm = (centred * lax.rsqrt(var + 1e-05) * gain_ref[...] + bias_ref[...]).astype(BF16)
        update = dot(onorm, w_ref[...], ((0,), (0,))) * gate_ref[half * SPAN : (half + 1) * SPAN]
        for j in range(HALF):
            tokens[pl.ds(half * HALF + j, ROWS, stride=COLS), :] = update[j * ROWS : (j + 1) * ROWS]
    out_ref[...] = tokens[...].astype(BF16)


def per_device(
    pair, pair_mask, in_gain, in_bias, proj_weight, gate_weight, out_gain, out_bias, out_weight
):
    shape = jax.ShapeDtypeStruct
    count = ROWS * COLS
    send, normed = call(
        factors_kernel,
        (shape((WIDTH, 2, 2 * SPAN), BF16), shape((count, WIDTH), BF16)),
        (pltpu.VMEM((count, WIDTH), F32), pltpu.VMEM((2 * SPAN // LANES, 2 * WIDTH, LANES), F32)),
        "factors",
    )(pair.reshape(count, WIDTH), pair_mask.T, in_gain[None], in_bias[None], proj_weight)
    exchange = functools.partial(
        lax.all_to_all, axis_name=AXES, split_axis=0, concat_axis=0, axis_index_groups=channel_groups(), tiled=True
    )
    both = exchange(send)
    gate = call(gate_kernel, shape((count, WIDTH), F32), name="gate")(normed, gate_weight)
    right = call(right_kernel, shape((4, JSPAN, SIDE), BF16), name="right")(both)
    right = lax.all_to_all(right, AXES, 0, 0, axis_index_groups=quad_groups(), tiled=True)
    left = call(left_kernel, shape((SIDE, SIDE), BF16), name="left")(both)
    other = lax.ppermute(left, AXES, core_swap())
    core = lax.rem(lax.axis_index("col"), 2).astype(jnp.int32).reshape(1)
    combined = pl.pallas_call(
        contract_kernel,
        out_shape=shape((RPOS * QPOS, 2, SPAN), BF16),
        in_specs=[pl.BlockSpec(memory_space=pltpu.VMEM)] * 3 + [pl.BlockSpec(memory_space=pltpu.SMEM)],
        scratch_shapes=[pltpu.VMEM((SIDE // LANES, SIDE, LANES), F32)],
        compiler_params=pltpu.CompilerParams(vmem_limit_bytes=16 * 2**20),
        name="contract",
    )(left, other, right, core)
    combined = exchange(combined)
    update = call(
        update_kernel,
        shape((count, WIDTH), BF16),
        (pltpu.VMEM((pl.cdiv(SPAN, LANES), 2 * WIDTH, LANES), F32), pltpu.VMEM((count, WIDTH), F32)),
        "update",
    )(combined, gate, out_gain[:, None], out_bias[:, None], out_weight)
    return update.reshape(ROWS, COLS, WIDTH)


def solution(mesh):
    return jax.shard_map(
        per_device,
        mesh=mesh,
        in_specs=(P("row", "col", None), P("row", "col"), P(), P(), P(), P(), P(), P(), P()),
        out_specs=P("row", "col", None),
        check_vma=False,
    )
```

```python
import functools

import jax
import jax.numpy as jnp
from jax import lax
from jax.experimental import pallas as pl
from jax.experimental.pallas import tpu as pltpu
from jax.sharding import PartitionSpec as P

BF16 = jnp.bfloat16
F32 = jnp.float32
AXES = ("row", "col")
ROWS, COLS, WIDTH = 48, 24, 128
WEIGHT = 100
HALF = COLS // 2
SPAN = HALF * ROWS
RPOS, QPOS = 8, 16
LANES = 128
SIDE = RPOS * ROWS
JSPAN = RPOS * COLS


def sigmoid(x):
    return 0.5 * jnp.tanh(0.5 * x) + 0.5


def device(z_hi, x, z_lo, y, core):
    return (z_hi * 4 + x) * 32 + z_lo * 16 + y * 2 + core


def x_of(side, x_low):
    return x_low if side == 0 else 3 - x_low


def positions():
    return [(zh, xl, zl, y) for zh in range(4) for xl in range(2) for zl in range(2) for y in range(8)]


def channel_groups():
    return [
        [device(zh, x_of(side, xl), zl, y, core) for zh, xl, zl, y in positions()]
        for side in range(2)
        for core in range(2)
    ]


def swap(mirror, core):
    return [
        (device(zh, x, zl, y, c), device(zh, 3 - x if mirror else x, zl, y, 1 - c if core else c))
        for zh in range(4)
        for x in range(4)
        for zl in range(2)
        for y in range(8)
        for c in range(2)
    ]


def dot(a, b, dims):
    return lax.dot_general(a, b, (dims, ((), ())), preferred_element_type=F32)


def call(kernel, out_shape, scratch=(), name=None):
    return pl.pallas_call(
        kernel,
        out_shape=out_shape,
        scratch_shapes=list(scratch),
        compiler_params=pltpu.CompilerParams(vmem_limit_bytes=16 * 2**20),
        name=name,
    )


def factors_kernel(*refs):
    given, (send_ref, normed_ref), held = refs[:5], refs[5:7], refs[7:12]
    tokens, pairs, sems = refs[12:]
    copies = [pltpu.make_async_copy(src, dst, sems.at[n]) for n, (src, dst) in enumerate(zip(given, held))]
    for copy in copies:
        copy.start()
    for copy in copies:
        copy.wait()
    x_ref, mask_ref, gain_ref, bias_ref, w_ref = held
    tokens[...] = x_ref[...].astype(F32)
    values = jnp.concatenate([tokens[pl.ds(k, ROWS, stride=COLS), :] for k in range(COLS)], axis=0)
    mean = jnp.mean(values, axis=-1, keepdims=True)
    centred = values - mean
    var = jnp.mean(centred * centred, axis=-1, keepdims=True)
    normed = (centred * lax.rsqrt(var + 1e-05) * gain_ref[...] + bias_ref[...]).astype(BF16)
    normed_ref[...] = normed
    token = lax.broadcasted_iota(jnp.int32, (ROWS, ROWS * COLS), 1)
    spread = (lax.rem(token, ROWS) == lax.broadcasted_iota(jnp.int32, token.shape, 0)).astype(BF16)
    every = dot(mask_ref[...].astype(F32).astype(BF16), spread, ((1,), (0,)))
    token = lax.broadcasted_iota(jnp.int32, every.shape, 1)
    first = lax.broadcasted_iota(jnp.int32, every.shape, 0) * ROWS
    mask = jnp.sum(jnp.where((token >= first) & (token < first + ROWS), every, 0.0), axis=0, keepdims=True)
    weight = w_ref[...].T
    for half in range(2):
        part = normed[half * SPAN : (half + 1) * SPAN]
        part_mask = mask[:, half * SPAN : (half + 1) * SPAN]
        sides = []
        for side in range(2):
            hidden = dot(weight[side * 2 * WIDTH : (side + 1) * 2 * WIDTH], part, ((1,), (1,)))
            sides.append(sigmoid(hidden[WIDTH:]) * hidden[:WIDTH] * part_mask)
        both = jnp.concatenate(sides, axis=1)
        for t in range(2 * SPAN // LANES):
            pairs[t, pl.ds(half, WIDTH, stride=2), :] = both[:, t * LANES : (t + 1) * LANES]
    for t in range(2 * SPAN // LANES):
        send_ref[:, :, t * LANES : (t + 1) * LANES] = pairs[t].astype(BF16).reshape(WIDTH, 2, LANES)


def gate_kernel(normed_ref, w_ref, gate_ref):
    gate_ref[...] = sigmoid(dot(normed_ref[...], w_ref[...], ((1,), (0,))))


def right_kernel(x_ref, core_ref, keep_ref, send_ref):
    x = x_ref[...].reshape(RPOS * QPOS * 2, 2 * SPAN)[:, SPAN:]
    core = core_ref[0]
    rows = 2 * QPOS
    for k in range(HALF // 2):
        blocks = [
            jnp.concatenate(
                [
                    x[rp * rows : (rp + 1) * rows, (h * 6 + k) * ROWS + b * COLS : (h * 6 + k) * ROWS + (b + 1) * COLS]
                    for h in range(2)
                    for rp in range(RPOS)
                ],
                axis=1,
            )
            for b in range(2)
        ]
        keep_ref[k * rows : (k + 1) * rows, :] = jnp.where(core == 0, blocks[0], blocks[1])
        send_ref[k * rows : (k + 1) * rows, :] = jnp.where(core == 0, blocks[1], blocks[0])


def left_kernel(x_ref, out_ref):
    x = x_ref[...].reshape(RPOS * QPOS * 2, 2 * SPAN)[:, :SPAN]
    rows = 2 * QPOS
    for k in range(HALF):
        out_ref[k * rows : (k + 1) * rows, :] = jnp.concatenate(
            [x[rp * rows : (rp + 1) * rows, k * ROWS : (k + 1) * ROWS] for rp in range(RPOS)], axis=1
        )


def product_kernel(left_ref, here_ref, mirror_ref, side_ref, total_ref):
    left = left_ref[...]
    for side, ref in ((side_ref[0], here_ref), (1 - side_ref[0], mirror_ref)):
        right = ref[...]
        part = jnp.zeros((JSPAN, SIDE), F32)
        for h in range(2):
            part += dot(right[:, h * JSPAN : (h + 1) * JSPAN], left[h * JSPAN : (h + 1) * JSPAN], ((0,), (0,)))
        for rp in range(RPOS):
            x = jnp.where(side == 0, rp % 2, 3 - rp % 2)
            rows = pl.ds(pl.multiple_of(((rp // 2) * 4 + x) * COLS, 8), COLS)
            for t in range(SIDE // LANES):
                total_ref[t, rows, :] = part[rp * COLS : (rp + 1) * COLS, t * LANES : (t + 1) * LANES]


def pack_kernel(here_ref, core_ref, send_ref, total):
    total[...] = here_ref[...] + core_ref[...]
    rows = 2 * QPOS
    blocks = [
        jnp.concatenate([total[t, pl.ds(j, rows, stride=HALF), :] for t in range(SIDE // LANES)], axis=1)
        for j in range(HALF)
    ]
    base = (functools.reduce(jnp.add, blocks) * (1.0 / HALF)).astype(BF16).astype(F32)
    blocks = [block - base for block in blocks] + [base]
    for rp in range(RPOS):
        piece = jnp.concatenate([block[:, rp * ROWS : (rp + 1) * ROWS] for block in blocks], axis=1)
        send_ref[rp * QPOS : (rp + 1) * QPOS] = piece.astype(BF16).reshape(QPOS, 2, SPAN + ROWS)


def update_kernel(x_ref, gate_ref, gain_ref, bias_ref, w_ref, out_ref, pairs, tokens):
    arrived = x_ref[...].reshape(2 * WIDTH, SPAN + ROWS).astype(F32)
    tiles = pl.cdiv(SPAN + ROWS, LANES)
    for t in range(tiles):
        tile = arrived[:, t * LANES : (t + 1) * LANES]
        pairs[t, :, : tile.shape[1]] = tile
    for half in range(2):
        values = [pairs[t, pl.ds(half, WIDTH, stride=2), :] for t in range(tiles)]
        values = jnp.concatenate(values, axis=1)
        base = values[:, SPAN : SPAN + ROWS]
        values = values[:, :SPAN] + jnp.concatenate([base] * HALF, axis=1)
        mean = jnp.mean(values, axis=0, keepdims=True)
        centred = values - mean
        var = jnp.mean(centred * centred, axis=0, keepdims=True)
        onorm = (centred * lax.rsqrt(var + 1e-05) * gain_ref[...] + bias_ref[...]).astype(BF16)
        update = dot(onorm, w_ref[...], ((0,), (0,))) * gate_ref[half * SPAN : (half + 1) * SPAN]
        for j in range(HALF):
            tokens[pl.ds(half * HALF + j, ROWS, stride=COLS), :] = update[j * ROWS : (j + 1) * ROWS]
    out_ref[...] = tokens[...].astype(BF16)


def per_device(
    pair, pair_mask, in_gain, in_bias, proj_weight, gate_weight, out_gain, out_bias, out_weight
):
    shape = jax.ShapeDtypeStruct
    count = ROWS * COLS
    given = pair.reshape(count, WIDTH), pair_mask.T, in_gain[None], in_bias[None], proj_weight
    send, normed = pl.pallas_call(
        factors_kernel,
        out_shape=(shape((WIDTH, 2, 2 * SPAN), BF16), shape((count, WIDTH), BF16)),
        in_specs=[pl.BlockSpec(memory_space=pl.ANY)] * 5,
        scratch_shapes=[pltpu.VMEM(value.shape, value.dtype) for value in given]
        + [
            pltpu.VMEM((count, WIDTH), F32),
            pltpu.VMEM((2 * SPAN // LANES, 2 * WIDTH, LANES), F32),
            pltpu.SemaphoreType.DMA((5,)),
        ],
        compiler_params=pltpu.CompilerParams(vmem_limit_bytes=56 * 2**20),
        name="factors",
    )(*given)
    exchange = functools.partial(
        lax.all_to_all, axis_name=AXES, split_axis=0, concat_axis=0, axis_index_groups=channel_groups(), tiled=True
    )
    core = lax.rem(lax.axis_index("col"), 2).astype(jnp.int32).reshape(1)
    side = (lax.rem(lax.axis_index("row"), 4) // 2).astype(jnp.int32).reshape(1)
    vmem, smem = pl.BlockSpec(memory_space=pltpu.VMEM), pl.BlockSpec(memory_space=pltpu.SMEM)
    both = exchange(send)
    gate = call(gate_kernel, shape((count, WIDTH), F32), name="gate")(normed, gate_weight)
    keep, away = pl.pallas_call(
        right_kernel,
        out_shape=(shape((JSPAN, SIDE), BF16),) * 2,
        in_specs=[vmem, smem],
        compiler_params=pltpu.CompilerParams(vmem_limit_bytes=16 * 2**20),
        name="right",
    )(both, core)
    away_mirror = lax.ppermute(away, AXES, swap(True, False))
    keep_mirror = lax.ppermute(keep, AXES, swap(True, False))
    left = call(left_kernel, shape((SIDE, SIDE), BF16), name="left")(both)
    product = functools.partial(
        pl.pallas_call,
        product_kernel,
        out_shape=shape((SIDE // LANES, SIDE, LANES), F32),
        in_specs=[vmem] * 3 + [smem],
        compiler_params=pltpu.CompilerParams(vmem_limit_bytes=16 * 2**20),
    )
    size = SIDE * SIDE * SIDE * 2
    partial = product(name="away", cost_estimate=pl.CostEstimate(flops=size, bytes_accessed=0, transcendentals=0))(
        left, away, away_mirror, side
    )
    partial = lax.ppermute(partial, AXES, swap(False, True))
    total = product(name="keep", cost_estimate=pl.CostEstimate(flops=size * WEIGHT, bytes_accessed=0, transcendentals=0))(
        left, keep, keep_mirror, side
    )
    combined = call(
        pack_kernel,
        shape((RPOS * QPOS, 2, SPAN + ROWS), BF16),
        (pltpu.VMEM((SIDE // LANES, SIDE, LANES), F32),),
        "pack",
    )(total, partial)
    combined = exchange(combined)
    update = call(
        update_kernel,
        shape((count, WIDTH), BF16),
        (pltpu.VMEM((pl.cdiv(SPAN + ROWS, LANES), 2 * WIDTH, LANES), F32), pltpu.VMEM((count, WIDTH), F32)),
        "update",
    )(combined, gate, out_gain[:, None], out_bias[:, None], out_weight)
    return update.reshape(ROWS, COLS, WIDTH)


def solution(mesh):
    return jax.shard_map(
        per_device,
        mesh=mesh,
        in_specs=(P("row", "col", None), P("row", "col"), P(), P(), P(), P(), P(), P(), P()),
        out_specs=P("row", "col", None),
        check_vma=False,
    )
```

```python
import functools

import jax
import jax.numpy as jnp
from jax import lax
from jax.experimental import pallas as pl
from jax.experimental.pallas import tpu as pltpu
from jax.sharding import PartitionSpec as P

BF16 = jnp.bfloat16
F32 = jnp.float32
AXES = ("row", "col")
ROWS, COLS, WIDTH = 48, 24, 128
COST_SCALE = 100
HALF = COLS // 2
SPAN = HALF * ROWS
RPOS, QPOS = 8, 16
LANES = 128
SIDE = RPOS * ROWS
JSPAN = RPOS * COLS


def sigmoid(x):
    return 0.5 * jnp.tanh(0.5 * x) + 0.5


def device(z_hi, x, z_lo, y, core):
    return (z_hi * 4 + x) * 32 + z_lo * 16 + y * 2 + core


def x_of(side, x_low):
    return x_low if side == 0 else 3 - x_low


def positions():
    return [(zh, xl, zl, y) for zh in range(4) for xl in range(2) for zl in range(2) for y in range(8)]


def channel_groups():
    return [
        [device(zh, x_of(side, xl), zl, y, core) for zh, xl, zl, y in positions()]
        for side in range(2)
        for core in range(2)
    ]


def swap(mirror, core):
    return [
        (device(zh, x, zl, y, c), device(zh, 3 - x if mirror else x, zl, y, 1 - c if core else c))
        for zh in range(4)
        for x in range(4)
        for zl in range(2)
        for y in range(8)
        for c in range(2)
    ]


def dot(a, b, dims):
    return lax.dot_general(a, b, (dims, ((), ())), preferred_element_type=F32)


def call(kernel, out_shape, scratch=(), name=None):
    return pl.pallas_call(
        kernel,
        out_shape=out_shape,
        scratch_shapes=list(scratch),
        compiler_params=pltpu.CompilerParams(vmem_limit_bytes=16 * 2**20),
        name=name,
    )


def factors_kernel(*refs):
    given, (send_ref, normed_ref), held = refs[:5], refs[5:7], refs[7:12]
    tokens, pairs, sems = refs[12:]
    copies = [pltpu.make_async_copy(src, dst, sems.at[n]) for n, (src, dst) in enumerate(zip(given, held))]
    for copy in copies:
        copy.start()
    for copy in copies:
        copy.wait()
    x_ref, mask_ref, gain_ref, bias_ref, w_ref = held
    tokens[...] = x_ref[...].astype(F32)
    values = jnp.concatenate([tokens[pl.ds(k, ROWS, stride=COLS), :] for k in range(COLS)], axis=0)
    mean = jnp.mean(values, axis=-1, keepdims=True)
    centred = values - mean
    var = jnp.mean(centred * centred, axis=-1, keepdims=True)
    normed = (centred * lax.rsqrt(var + 1e-05) * gain_ref[...] + bias_ref[...]).astype(BF16)
    normed_ref[...] = normed
    token = lax.broadcasted_iota(jnp.int32, (ROWS, ROWS * COLS), 1)
    spread = (lax.rem(token, ROWS) == lax.broadcasted_iota(jnp.int32, token.shape, 0)).astype(BF16)
    every = dot(mask_ref[...].astype(F32).astype(BF16), spread, ((1,), (0,)))
    token = lax.broadcasted_iota(jnp.int32, every.shape, 1)
    first = lax.broadcasted_iota(jnp.int32, every.shape, 0) * ROWS
    mask = jnp.sum(jnp.where((token >= first) & (token < first + ROWS), every, 0.0), axis=0, keepdims=True)
    weight = w_ref[...].T
    for half in range(2):
        part = normed[half * SPAN : (half + 1) * SPAN]
        part_mask = mask[:, half * SPAN : (half + 1) * SPAN]
        sides = []
        for side in range(2):
            hidden = dot(weight[side * 2 * WIDTH : (side + 1) * 2 * WIDTH], part, ((1,), (1,)))
            sides.append(sigmoid(hidden[WIDTH:]) * hidden[:WIDTH] * part_mask)
        both = jnp.concatenate(sides, axis=1)
        for t in range(2 * SPAN // LANES):
            pairs[t, pl.ds(half, WIDTH, stride=2), :] = both[:, t * LANES : (t + 1) * LANES]
    for t in range(2 * SPAN // LANES):
        send_ref[:, :, t * LANES : (t + 1) * LANES] = pairs[t].astype(BF16).reshape(WIDTH, 2, LANES)


def gate_kernel(normed_ref, w_ref, gate_ref):
    gate_ref[...] = sigmoid(dot(normed_ref[...], w_ref[...], ((1,), (0,))))


def right_kernel(x_ref, core_ref, keep_ref, send_ref):
    x = x_ref[...].reshape(RPOS * QPOS * 2, 2 * SPAN)[:, SPAN:]
    core = core_ref[0]
    rows = 2 * QPOS
    for k in range(HALF // 2):
        blocks = [
            jnp.concatenate(
                [
                    x[rp * rows : (rp + 1) * rows, (h * 6 + k) * ROWS + b * COLS : (h * 6 + k) * ROWS + (b + 1) * COLS]
                    for h in range(2)
                    for rp in range(RPOS)
                ],
                axis=1,
            )
            for b in range(2)
        ]
        keep_ref[k * rows : (k + 1) * rows, :] = jnp.where(core == 0, blocks[0], blocks[1])
        send_ref[k * rows : (k + 1) * rows, :] = jnp.where(core == 0, blocks[1], blocks[0])


def left_kernel(x_ref, away_ref, out_ref):
    x = x_ref[...].reshape(RPOS * QPOS * 2, 2 * SPAN)[:, :SPAN]
    rows = 2 * QPOS
    for k in range(HALF):
        out_ref[k * rows : (k + 1) * rows, :] = jnp.concatenate(
            [x[rp * rows : (rp + 1) * rows, k * ROWS : (k + 1) * ROWS] for rp in range(RPOS)], axis=1
        )
    out_ref[SIDE:, :] = away_ref[...]


def add_products(left, here, mirror, side, total, earlier=None):
    for at, right in ((side, here), (1 - side, mirror)):
        part = jnp.zeros((JSPAN, SIDE), F32)
        for h in range(2):
            part += dot(right[:, h * JSPAN : (h + 1) * JSPAN], left[h * JSPAN : (h + 1) * JSPAN], ((0,), (0,)))
        for rp in range(RPOS):
            x = jnp.where(at == 0, rp % 2, 3 - rp % 2)
            rows = pl.ds(pl.multiple_of(((rp // 2) * 4 + x) * COLS, 8), COLS)
            for t in range(SIDE // LANES):
                piece = part[rp * COLS : (rp + 1) * COLS, t * LANES : (t + 1) * LANES]
                total[t, rows, :] = piece if earlier is None else piece + earlier[t, rows, :]


def own_kernel(bundle_ref, keep_ref, mirror_ref, side_ref, total_ref):
    add_products(bundle_ref[:SIDE], keep_ref[...], mirror_ref[...], side_ref[0], total_ref)


def contract_kernel(bundle_ref, cross_ref, own_ref, side_ref, send_ref, total):
    add_products(bundle_ref[:SIDE], bundle_ref[SIDE:], cross_ref[...], side_ref[0], total, own_ref)
    rows = 2 * QPOS
    blocks = [
        jnp.concatenate([total[t, pl.ds(j, rows, stride=HALF), :] for t in range(SIDE // LANES)], axis=1)
        for j in range(HALF)
    ]
    base = (functools.reduce(jnp.add, blocks) * (1.0 / HALF)).astype(BF16).astype(F32)
    blocks = [block - base for block in blocks] + [base]
    for rp in range(RPOS):
        piece = jnp.concatenate([block[:, rp * ROWS : (rp + 1) * ROWS] for block in blocks], axis=1)
        send_ref[rp * QPOS : (rp + 1) * QPOS] = piece.astype(BF16).reshape(QPOS, 2, SPAN + ROWS)


def update_kernel(x_ref, gate_ref, gain_ref, bias_ref, w_ref, out_ref, pairs, tokens):
    arrived = x_ref[...].reshape(2 * WIDTH, SPAN + ROWS).astype(F32)
    tiles = pl.cdiv(SPAN + ROWS, LANES)
    for t in range(tiles):
        tile = arrived[:, t * LANES : (t + 1) * LANES]
        pairs[t, :, : tile.shape[1]] = tile
    for half in range(2):
        values = [pairs[t, pl.ds(half, WIDTH, stride=2), :] for t in range(tiles)]
        values = jnp.concatenate(values, axis=1)
        base = values[:, SPAN : SPAN + ROWS]
        values = values[:, :SPAN] + jnp.concatenate([base] * HALF, axis=1)
        mean = jnp.mean(values, axis=0, keepdims=True)
        centred = values - mean
        var = jnp.mean(centred * centred, axis=0, keepdims=True)
        onorm = (centred * lax.rsqrt(var + 1e-05) * gain_ref[...] + bias_ref[...]).astype(BF16)
        update = dot(onorm, w_ref[...], ((0,), (0,))) * gate_ref[half * SPAN : (half + 1) * SPAN]
        for j in range(HALF):
            tokens[pl.ds(half * HALF + j, ROWS, stride=COLS), :] = update[j * ROWS : (j + 1) * ROWS]
    out_ref[...] = tokens[...].astype(BF16)


def per_device(
    pair, pair_mask, in_gain, in_bias, proj_weight, gate_weight, out_gain, out_bias, out_weight
):
    shape = jax.ShapeDtypeStruct
    count = ROWS * COLS
    given = pair.reshape(count, WIDTH), pair_mask.T, in_gain[None], in_bias[None], proj_weight
    send, normed = pl.pallas_call(
        factors_kernel,
        out_shape=(shape((WIDTH, 2, 2 * SPAN), BF16), shape((count, WIDTH), BF16)),
        in_specs=[pl.BlockSpec(memory_space=pl.ANY)] * 5,
        scratch_shapes=[pltpu.VMEM(value.shape, value.dtype) for value in given]
        + [
            pltpu.VMEM((count, WIDTH), F32),
            pltpu.VMEM((2 * SPAN // LANES, 2 * WIDTH, LANES), F32),
            pltpu.SemaphoreType.DMA((5,)),
        ],
        compiler_params=pltpu.CompilerParams(vmem_limit_bytes=56 * 2**20),
        name="factors",
    )(*given)
    exchange = functools.partial(
        lax.all_to_all, axis_name=AXES, split_axis=0, concat_axis=0, axis_index_groups=channel_groups(), tiled=True
    )
    core = lax.rem(lax.axis_index("col"), 2).astype(jnp.int32).reshape(1)
    side = (lax.rem(lax.axis_index("row"), 4) // 2).astype(jnp.int32).reshape(1)
    vmem, smem = pl.BlockSpec(memory_space=pltpu.VMEM), pl.BlockSpec(memory_space=pltpu.SMEM)
    both = exchange(send)
    gate = call(gate_kernel, shape((count, WIDTH), F32), name="gate")(normed, gate_weight)
    keep, away = pl.pallas_call(
        right_kernel,
        out_shape=(shape((JSPAN, SIDE), BF16),) * 2,
        in_specs=[vmem, smem],
        compiler_params=pltpu.CompilerParams(vmem_limit_bytes=16 * 2**20),
        name="right",
    )(both, core)
    mirror = lax.ppermute(keep, AXES, swap(True, False))
    cross = lax.ppermute(away, AXES, swap(True, True))
    bundle = call(left_kernel, shape((SIDE + JSPAN, SIDE), BF16), name="left")(both, away)
    bundle_core = lax.ppermute(bundle, AXES, swap(False, True))
    own = pl.pallas_call(
        own_kernel,
        out_shape=shape((SIDE // LANES, SIDE, LANES), F32),
        in_specs=[vmem] * 3 + [smem],
        compiler_params=pltpu.CompilerParams(vmem_limit_bytes=16 * 2**20),
        cost_estimate=pl.CostEstimate(flops=SIDE * SIDE * SIDE * 2 * COST_SCALE, bytes_accessed=0, transcendentals=0),
        name="own",
    )(bundle, keep, mirror, side)
    combined = pl.pallas_call(
        contract_kernel,
        out_shape=shape((RPOS * QPOS, 2, SPAN + ROWS), BF16),
        in_specs=[vmem] * 3 + [smem],
        scratch_shapes=[pltpu.VMEM((SIDE // LANES, SIDE, LANES), F32)],
        compiler_params=pltpu.CompilerParams(vmem_limit_bytes=16 * 2**20),
        name="contract",
    )(bundle_core, cross, own, side)
    combined = exchange(combined)
    update = call(
        update_kernel,
        shape((count, WIDTH), BF16),
        (pltpu.VMEM((pl.cdiv(SPAN + ROWS, LANES), 2 * WIDTH, LANES), F32), pltpu.VMEM((count, WIDTH), F32)),
        "update",
    )(combined, gate, out_gain[:, None], out_bias[:, None], out_weight)
    return update.reshape(ROWS, COLS, WIDTH)


def solution(mesh):
    return jax.shard_map(
        per_device,
        mesh=mesh,
        in_specs=(P("row", "col", None), P("row", "col"), P(), P(), P(), P(), P(), P(), P()),
        out_specs=P("row", "col", None),
        check_vma=False,
    )
```

```python
import functools

import jax
import jax.numpy as jnp
from jax import lax
from jax.experimental import pallas as pl
from jax.experimental.pallas import tpu as pltpu
from jax.sharding import PartitionSpec as P

BF16 = jnp.bfloat16
F32 = jnp.float32
AXES = ("row", "col")
ROWS, COLS, WIDTH = 48, 24, 128
COST_SCALE = 100
HALF = COLS // 2
SPAN = HALF * ROWS
RPOS, QPOS = 8, 16
LANES = 128
SIDE = RPOS * ROWS
JSPAN = RPOS * COLS


def sigmoid(x):
    return 0.5 * jnp.tanh(0.5 * x) + 0.5


def device(z_hi, x, z_lo, y, core):
    return (z_hi * 4 + x) * 32 + z_lo * 16 + y * 2 + core


def x_of(side, x_low):
    return x_low if side == 0 else 3 - x_low


def positions():
    return [(zh, xl, zl, y) for zh in range(4) for xl in range(2) for zl in range(2) for y in range(8)]


def channel_groups():
    return [
        [device(zh, x_of(side, xl), zl, y, core) for zh, xl, zl, y in positions()]
        for side in range(2)
        for core in range(2)
    ]


def swap(mirror, core):
    return [
        (device(zh, x, zl, y, c), device(zh, 3 - x if mirror else x, zl, y, 1 - c if core else c))
        for zh in range(4)
        for x in range(4)
        for zl in range(2)
        for y in range(8)
        for c in range(2)
    ]


def dot(a, b, dims):
    return lax.dot_general(a, b, (dims, ((), ())), preferred_element_type=F32)


def call(kernel, out_shape, scratch=(), name=None):
    return pl.pallas_call(
        kernel,
        out_shape=out_shape,
        scratch_shapes=list(scratch),
        compiler_params=pltpu.CompilerParams(vmem_limit_bytes=16 * 2**20),
        name=name,
    )


def factors_kernel(*refs):
    given, (send_ref, normed_ref), held = refs[:5], refs[5:7], refs[7:12]
    tokens, pairs, sems = refs[12:]
    copies = [pltpu.make_async_copy(src, dst, sems.at[n]) for n, (src, dst) in enumerate(zip(given, held))]
    for copy in copies:
        copy.start()
    for copy in copies:
        copy.wait()
    x_ref, mask_ref, gain_ref, bias_ref, w_ref = held
    tokens[...] = x_ref[...].astype(F32)
    values = jnp.concatenate([tokens[pl.ds(k, ROWS, stride=COLS), :] for k in range(COLS)], axis=0)
    mean = jnp.mean(values, axis=-1, keepdims=True)
    centred = values - mean
    var = jnp.mean(centred * centred, axis=-1, keepdims=True)
    normed = (centred * lax.rsqrt(var + 1e-05) * gain_ref[...] + bias_ref[...]).astype(BF16)
    normed_ref[...] = normed
    token = lax.broadcasted_iota(jnp.int32, (ROWS, ROWS * COLS), 1)
    spread = (lax.rem(token, ROWS) == lax.broadcasted_iota(jnp.int32, token.shape, 0)).astype(BF16)
    every = dot(mask_ref[...].astype(F32).astype(BF16), spread, ((1,), (0,)))
    token = lax.broadcasted_iota(jnp.int32, every.shape, 1)
    first = lax.broadcasted_iota(jnp.int32, every.shape, 0) * ROWS
    mask = jnp.sum(jnp.where((token >= first) & (token < first + ROWS), every, 0.0), axis=0, keepdims=True)
    weight = w_ref[...].T
    for half in range(2):
        part = normed[half * SPAN : (half + 1) * SPAN]
        part_mask = mask[:, half * SPAN : (half + 1) * SPAN]
        sides = []
        for side in range(2):
            hidden = dot(weight[side * 2 * WIDTH : (side + 1) * 2 * WIDTH], part, ((1,), (1,)))
            sides.append(sigmoid(hidden[WIDTH:]) * hidden[:WIDTH] * part_mask)
        both = jnp.concatenate(sides, axis=1)
        for t in range(2 * SPAN // LANES):
            pairs[t, pl.ds(half, WIDTH, stride=2), :] = both[:, t * LANES : (t + 1) * LANES]
    for t in range(2 * SPAN // LANES):
        send_ref[:, :, t * LANES : (t + 1) * LANES] = pairs[t].astype(BF16).reshape(WIDTH, 2, LANES)


def gate_kernel(normed_ref, w_ref, *rest_refs):
    *from_refs, gate_ref, gain_ref, bias_ref, out_w_ref = rest_refs
    gate_ref[...] = sigmoid(dot(normed_ref[...], w_ref[...], ((1,), (0,))))
    for source, target in zip(from_refs, (gain_ref, bias_ref, out_w_ref)):
        target[...] = source[...]


def right_kernel(x_ref, core_ref, keep_ref, send_ref):
    x = x_ref[...].reshape(RPOS * QPOS * 2, 2 * SPAN)[:, SPAN:]
    core = core_ref[0]
    rows = 2 * QPOS
    for k in range(HALF // 2):
        blocks = [
            jnp.concatenate(
                [
                    x[rp * rows : (rp + 1) * rows, (h * 6 + k) * ROWS + b * COLS : (h * 6 + k) * ROWS + (b + 1) * COLS]
                    for h in range(2)
                    for rp in range(RPOS)
                ],
                axis=1,
            )
            for b in range(2)
        ]
        keep_ref[k * rows : (k + 1) * rows, :] = jnp.where(core == 0, blocks[0], blocks[1])
        send_ref[k * rows : (k + 1) * rows, :] = jnp.where(core == 0, blocks[1], blocks[0])


def left_kernel(x_ref, away_ref, out_ref):
    x = x_ref[...].reshape(RPOS * QPOS * 2, 2 * SPAN)[:, :SPAN]
    rows = 2 * QPOS
    for k in range(HALF):
        out_ref[k * rows : (k + 1) * rows, :] = jnp.concatenate(
            [x[rp * rows : (rp + 1) * rows, k * ROWS : (k + 1) * ROWS] for rp in range(RPOS)], axis=1
        )
    out_ref[SIDE:, :] = away_ref[...]


def add_products(left, here, mirror, side, total, earlier=None):
    for at, right in ((side, here), (1 - side, mirror)):
        part = jnp.zeros((JSPAN, SIDE), F32)
        for h in range(2):
            part += dot(right[:, h * JSPAN : (h + 1) * JSPAN], left[h * JSPAN : (h + 1) * JSPAN], ((0,), (0,)))
        for rp in range(RPOS):
            x = jnp.where(at == 0, rp % 2, 3 - rp % 2)
            rows = pl.ds(pl.multiple_of(((rp // 2) * 4 + x) * COLS, 8), COLS)
            for t in range(SIDE // LANES):
                piece = part[rp * COLS : (rp + 1) * COLS, t * LANES : (t + 1) * LANES]
                total[t, rows, :] = piece if earlier is None else piece + earlier[t, rows, :]


def own_kernel(bundle_ref, keep_ref, mirror_ref, side_ref, total_ref):
    add_products(bundle_ref[:SIDE], keep_ref[...], mirror_ref[...], side_ref[0], total_ref)


def contract_kernel(bundle_ref, cross_ref, own_ref, side_ref, send_ref, total):
    add_products(bundle_ref[:SIDE], bundle_ref[SIDE:], cross_ref[...], side_ref[0], total, own_ref)
    rows = 2 * QPOS
    blocks = [
        jnp.concatenate([total[t, pl.ds(j, rows, stride=HALF), :] for t in range(SIDE // LANES)], axis=1)
        for j in range(HALF)
    ]
    base = (functools.reduce(jnp.add, blocks) * (1.0 / HALF)).astype(BF16).astype(F32)
    blocks = [block - base for block in blocks] + [base]
    for rp in range(RPOS):
        piece = jnp.concatenate([block[:, rp * ROWS : (rp + 1) * ROWS] for block in blocks], axis=1)
        send_ref[rp * QPOS : (rp + 1) * QPOS] = piece.astype(BF16).reshape(QPOS, 2, SPAN + ROWS)


def update_kernel(x_ref, gate_ref, gain_ref, bias_ref, w_ref, out_ref, pairs, tokens):
    arrived = x_ref[...].reshape(2 * WIDTH, SPAN + ROWS).astype(F32)
    tiles = pl.cdiv(SPAN + ROWS, LANES)
    for t in range(tiles):
        tile = arrived[:, t * LANES : (t + 1) * LANES]
        pairs[t, :, : tile.shape[1]] = tile
    for half in range(2):
        values = [pairs[t, pl.ds(half, WIDTH, stride=2), :] for t in range(tiles)]
        values = jnp.concatenate(values, axis=1)
        base = values[:, SPAN : SPAN + ROWS]
        values = values[:, :SPAN] + jnp.concatenate([base] * HALF, axis=1)
        mean = jnp.mean(values, axis=0, keepdims=True)
        centred = values - mean
        var = jnp.mean(centred * centred, axis=0, keepdims=True)
        onorm = (centred * lax.rsqrt(var + 1e-05) * gain_ref[...] + bias_ref[...]).astype(BF16)
        update = dot(onorm, w_ref[...], ((0,), (0,))) * gate_ref[half * SPAN : (half + 1) * SPAN]
        for j in range(HALF):
            tokens[pl.ds(half * HALF + j, ROWS, stride=COLS), :] = update[j * ROWS : (j + 1) * ROWS]
    out_ref[...] = tokens[...].astype(BF16)


def per_device(
    pair, pair_mask, in_gain, in_bias, proj_weight, gate_weight, out_gain, out_bias, out_weight
):
    shape = jax.ShapeDtypeStruct
    count = ROWS * COLS
    given = pair.reshape(count, WIDTH), pair_mask.T, in_gain[None], in_bias[None], proj_weight
    send, normed = pl.pallas_call(
        factors_kernel,
        out_shape=(shape((WIDTH, 2, 2 * SPAN), BF16), shape((count, WIDTH), BF16)),
        in_specs=[pl.BlockSpec(memory_space=pl.ANY)] * 5,
        scratch_shapes=[pltpu.VMEM(value.shape, value.dtype) for value in given]
        + [
            pltpu.VMEM((count, WIDTH), F32),
            pltpu.VMEM((2 * SPAN // LANES, 2 * WIDTH, LANES), F32),
            pltpu.SemaphoreType.DMA((5,)),
        ],
        compiler_params=pltpu.CompilerParams(vmem_limit_bytes=56 * 2**20),
        name="factors",
    )(*given)
    exchange = functools.partial(
        lax.all_to_all, axis_name=AXES, split_axis=0, concat_axis=0, axis_index_groups=channel_groups(), tiled=True
    )
    core = lax.rem(lax.axis_index("col"), 2).astype(jnp.int32).reshape(1)
    side = (lax.rem(lax.axis_index("row"), 4) // 2).astype(jnp.int32).reshape(1)
    vmem, smem = pl.BlockSpec(memory_space=pltpu.VMEM), pl.BlockSpec(memory_space=pltpu.SMEM)
    both = exchange(send)
    last = out_gain[:, None], out_bias[:, None], out_weight
    late = call(
        gate_kernel, [shape((count, WIDTH), F32)] + [shape(value.shape, value.dtype) for value in last], name="gate"
    )(normed, gate_weight, *last)
    late, both = lax.optimization_barrier((late, both))
    keep, away = pl.pallas_call(
        right_kernel,
        out_shape=(shape((JSPAN, SIDE), BF16),) * 2,
        in_specs=[vmem, smem],
        compiler_params=pltpu.CompilerParams(vmem_limit_bytes=16 * 2**20),
        name="right",
    )(both, core)
    mirror = lax.ppermute(keep, AXES, swap(True, False))
    cross = lax.ppermute(away, AXES, swap(True, True))
    bundle = call(left_kernel, shape((SIDE + JSPAN, SIDE), BF16), name="left")(both, away)
    bundle_core = lax.ppermute(bundle, AXES, swap(False, True))
    own = pl.pallas_call(
        own_kernel,
        out_shape=shape((SIDE // LANES, SIDE, LANES), F32),
        in_specs=[vmem] * 3 + [smem],
        compiler_params=pltpu.CompilerParams(vmem_limit_bytes=16 * 2**20),
        cost_estimate=pl.CostEstimate(flops=SIDE * SIDE * SIDE * 2 * COST_SCALE, bytes_accessed=0, transcendentals=0),
        name="own",
    )(bundle, keep, mirror, side)
    combined = pl.pallas_call(
        contract_kernel,
        out_shape=shape((RPOS * QPOS, 2, SPAN + ROWS), BF16),
        in_specs=[vmem] * 3 + [smem],
        scratch_shapes=[pltpu.VMEM((SIDE // LANES, SIDE, LANES), F32)],
        compiler_params=pltpu.CompilerParams(vmem_limit_bytes=16 * 2**20),
        name="contract",
    )(bundle_core, cross, own, side)
    combined = exchange(combined)
    update = call(
        update_kernel,
        shape((count, WIDTH), BF16),
        (pltpu.VMEM((pl.cdiv(SPAN + ROWS, LANES), 2 * WIDTH, LANES), F32), pltpu.VMEM((count, WIDTH), F32)),
        "update",
    )(combined, *late)
    return update.reshape(ROWS, COLS, WIDTH)


def solution(mesh):
    return jax.shard_map(
        per_device,
        mesh=mesh,
        in_specs=(P("row", "col", None), P("row", "col"), P(), P(), P(), P(), P(), P(), P()),
        out_specs=P("row", "col", None),
        check_vma=False,
    )
```

```python
import functools

import jax
import jax.numpy as jnp
from jax import lax
from jax.experimental import pallas as pl
from jax.experimental.pallas import tpu as pltpu
from jax.sharding import PartitionSpec as P

BF16 = jnp.bfloat16
F32 = jnp.float32
AXES = ("row", "col")
ROWS, COLS, WIDTH = 48, 24, 128
COST_SCALE = 100
HALF = COLS // 2
SPAN = HALF * ROWS
RPOS, QPOS = 8, 16
LANES = 128
SIDE = RPOS * ROWS
JSPAN = RPOS * COLS


def sigmoid(x):
    return 0.5 * jnp.tanh(0.5 * x) + 0.5


def device(z_hi, x, z_lo, y, core):
    return (z_hi * 4 + x) * 32 + z_lo * 16 + y * 2 + core


def x_of(side, x_low):
    return x_low if side == 0 else 3 - x_low


def lead(items, start):
    return items[start:] + items[:start]


ROW_ORDER = lead([(zh, xl) for zh in range(4) for xl in range(2)], 4)
COL_ORDER = lead([(zl, y) for zl in range(2) for y in range(8)], 12)


def positions():
    return [(zh, xl, zl, y) for zh, xl in ROW_ORDER for zl, y in COL_ORDER]


def column_position(z_hi, x):
    row = z_hi * 4 + x
    return COL_ORDER.index((row // 8, row % 8))


def channel_groups():
    return [
        [device(zh, x_of(side, xl), zl, y, core) for zh, xl, zl, y in positions()]
        for side in range(2)
        for core in range(2)
    ]


def swap(mirror, core):
    return [
        (device(zh, x, zl, y, c), device(zh, 3 - x if mirror else x, zl, y, 1 - c if core else c))
        for zh in range(4)
        for x in range(4)
        for zl in range(2)
        for y in range(8)
        for c in range(2)
    ]


def dot(a, b, dims):
    return lax.dot_general(a, b, (dims, ((), ())), preferred_element_type=F32)


def call(kernel, out_shape, scratch=(), name=None):
    return pl.pallas_call(
        kernel,
        out_shape=out_shape,
        scratch_shapes=list(scratch),
        compiler_params=pltpu.CompilerParams(vmem_limit_bytes=16 * 2**20),
        name=name,
    )


def factors_kernel(*refs):
    given, (send_ref, normed_ref), held = refs[:5], refs[5:7], refs[7:12]
    tokens, pairs, sems = refs[12:]
    copies = [pltpu.make_async_copy(src, dst, sems.at[n]) for n, (src, dst) in enumerate(zip(given, held))]
    for copy in copies:
        copy.start()
    for copy in copies:
        copy.wait()
    x_ref, mask_ref, gain_ref, bias_ref, w_ref = held
    tokens[...] = x_ref[...].astype(F32)
    values = jnp.concatenate([tokens[pl.ds(k, ROWS, stride=COLS), :] for k in range(COLS)], axis=0)
    mean = jnp.mean(values, axis=-1, keepdims=True)
    centred = values - mean
    var = jnp.mean(centred * centred, axis=-1, keepdims=True)
    normed = (centred * lax.rsqrt(var + 1e-05) * gain_ref[...] + bias_ref[...]).astype(BF16)
    normed_ref[...] = normed
    token = lax.broadcasted_iota(jnp.int32, (ROWS, ROWS * COLS), 1)
    spread = (lax.rem(token, ROWS) == lax.broadcasted_iota(jnp.int32, token.shape, 0)).astype(BF16)
    every = dot(mask_ref[...].astype(F32).astype(BF16), spread, ((1,), (0,)))
    token = lax.broadcasted_iota(jnp.int32, every.shape, 1)
    first = lax.broadcasted_iota(jnp.int32, every.shape, 0) * ROWS
    mask = jnp.sum(jnp.where((token >= first) & (token < first + ROWS), every, 0.0), axis=0, keepdims=True)
    weight = w_ref[...].T
    for half in range(2):
        part = normed[half * SPAN : (half + 1) * SPAN]
        part_mask = mask[:, half * SPAN : (half + 1) * SPAN]
        sides = []
        for side in range(2):
            hidden = dot(weight[side * 2 * WIDTH : (side + 1) * 2 * WIDTH], part, ((1,), (1,)))
            sides.append(sigmoid(hidden[WIDTH:]) * hidden[:WIDTH] * part_mask)
        both = jnp.concatenate(sides, axis=1)
        for t in range(2 * SPAN // LANES):
            pairs[t, pl.ds(half, WIDTH, stride=2), :] = both[:, t * LANES : (t + 1) * LANES]
    for t in range(2 * SPAN // LANES):
        send_ref[:, :, t * LANES : (t + 1) * LANES] = pairs[t].astype(BF16).reshape(WIDTH, 2, LANES)


def gate_kernel(normed_ref, w_ref, *rest_refs):
    *from_refs, gate_ref, gain_ref, bias_ref, out_w_ref = rest_refs
    gate_ref[...] = sigmoid(dot(normed_ref[...], w_ref[...], ((1,), (0,))))
    for source, target in zip(from_refs, (gain_ref, bias_ref, out_w_ref)):
        target[...] = source[...]


def right_kernel(x_ref, core_ref, keep_ref, send_ref):
    x = x_ref[...].reshape(RPOS * QPOS * 2, 2 * SPAN)[:, SPAN:]
    core = core_ref[0]
    rows = 2 * QPOS
    for k in range(HALF // 2):
        blocks = [
            jnp.concatenate(
                [
                    x[rp * rows : (rp + 1) * rows, (h * 6 + k) * ROWS + b * COLS : (h * 6 + k) * ROWS + (b + 1) * COLS]
                    for h in range(2)
                    for rp in range(RPOS)
                ],
                axis=1,
            )
            for b in range(2)
        ]
        keep_ref[k * rows : (k + 1) * rows, :] = jnp.where(core == 0, blocks[0], blocks[1])
        send_ref[k * rows : (k + 1) * rows, :] = jnp.where(core == 0, blocks[1], blocks[0])


def left_kernel(x_ref, away_ref, out_ref):
    x = x_ref[...].reshape(RPOS * QPOS * 2, 2 * SPAN)[:, :SPAN]
    rows = 2 * QPOS
    for k in range(HALF):
        out_ref[k * rows : (k + 1) * rows, :] = jnp.concatenate(
            [x[rp * rows : (rp + 1) * rows, k * ROWS : (k + 1) * ROWS] for rp in range(RPOS)], axis=1
        )
    out_ref[SIDE:, :] = away_ref[...]


def add_products(left, here, mirror, side, total, earlier=None):
    for at, right in ((side, here), (1 - side, mirror)):
        part = jnp.zeros((JSPAN, SIDE), F32)
        for h in range(2):
            part += dot(right[:, h * JSPAN : (h + 1) * JSPAN], left[h * JSPAN : (h + 1) * JSPAN], ((0,), (0,)))
        for rp, (z_hi, x_low) in enumerate(ROW_ORDER):
            places = [column_position(z_hi, x_of(s, x_low)) * COLS for s in range(2)]
            rows = pl.ds(pl.multiple_of(jnp.where(at == 0, places[0], places[1]), 8), COLS)
            for t in range(SIDE // LANES):
                piece = part[rp * COLS : (rp + 1) * COLS, t * LANES : (t + 1) * LANES]
                total[t, rows, :] = piece if earlier is None else piece + earlier[t, rows, :]


def own_kernel(bundle_ref, keep_ref, mirror_ref, side_ref, total_ref):
    add_products(bundle_ref[:SIDE], keep_ref[...], mirror_ref[...], side_ref[0], total_ref)


def contract_kernel(bundle_ref, cross_ref, own_ref, side_ref, send_ref, total):
    add_products(bundle_ref[:SIDE], bundle_ref[SIDE:], cross_ref[...], side_ref[0], total, own_ref)
    rows = 2 * QPOS
    blocks = [
        jnp.concatenate([total[t, pl.ds(j, rows, stride=HALF), :] for t in range(SIDE // LANES)], axis=1)
        for j in range(HALF)
    ]
    base = (functools.reduce(jnp.add, blocks) * (1.0 / HALF)).astype(BF16).astype(F32)
    blocks = [block - base for block in blocks] + [base]
    for rp in range(RPOS):
        piece = jnp.concatenate([block[:, rp * ROWS : (rp + 1) * ROWS] for block in blocks], axis=1)
        send_ref[rp * QPOS : (rp + 1) * QPOS] = piece.astype(BF16).reshape(QPOS, 2, SPAN + ROWS)


def update_kernel(x_ref, gate_ref, gain_ref, bias_ref, w_ref, out_ref, pairs, tokens):
    arrived = x_ref[...].reshape(2 * WIDTH, SPAN + ROWS).astype(F32)
    tiles = pl.cdiv(SPAN + ROWS, LANES)
    for t in range(tiles):
        tile = arrived[:, t * LANES : (t + 1) * LANES]
        pairs[t, :, : tile.shape[1]] = tile
    for half in range(2):
        values = [pairs[t, pl.ds(half, WIDTH, stride=2), :] for t in range(tiles)]
        values = jnp.concatenate(values, axis=1)
        base = values[:, SPAN : SPAN + ROWS]
        values = values[:, :SPAN] + jnp.concatenate([base] * HALF, axis=1)
        mean = jnp.mean(values, axis=0, keepdims=True)
        centred = values - mean
        var = jnp.mean(centred * centred, axis=0, keepdims=True)
        onorm = (centred * lax.rsqrt(var + 1e-05) * gain_ref[...] + bias_ref[...]).astype(BF16)
        update = dot(onorm, w_ref[...], ((0,), (0,))) * gate_ref[half * SPAN : (half + 1) * SPAN]
        for j in range(HALF):
            tokens[pl.ds(half * HALF + j, ROWS, stride=COLS), :] = update[j * ROWS : (j + 1) * ROWS]
    out_ref[...] = tokens[...].astype(BF16)


def per_device(
    pair, pair_mask, in_gain, in_bias, proj_weight, gate_weight, out_gain, out_bias, out_weight
):
    shape = jax.ShapeDtypeStruct
    count = ROWS * COLS
    given = pair.reshape(count, WIDTH), pair_mask.T, in_gain[None], in_bias[None], proj_weight
    send, normed = pl.pallas_call(
        factors_kernel,
        out_shape=(shape((WIDTH, 2, 2 * SPAN), BF16), shape((count, WIDTH), BF16)),
        in_specs=[pl.BlockSpec(memory_space=pl.ANY)] * 5,
        scratch_shapes=[pltpu.VMEM(value.shape, value.dtype) for value in given]
        + [
            pltpu.VMEM((count, WIDTH), F32),
            pltpu.VMEM((2 * SPAN // LANES, 2 * WIDTH, LANES), F32),
            pltpu.SemaphoreType.DMA((5,)),
        ],
        compiler_params=pltpu.CompilerParams(vmem_limit_bytes=56 * 2**20),
        name="factors",
    )(*given)
    exchange = functools.partial(
        lax.all_to_all, axis_name=AXES, split_axis=0, concat_axis=0, axis_index_groups=channel_groups(), tiled=True
    )
    core = lax.rem(lax.axis_index("col"), 2).astype(jnp.int32).reshape(1)
    side = (lax.rem(lax.axis_index("row"), 4) // 2).astype(jnp.int32).reshape(1)
    vmem, smem = pl.BlockSpec(memory_space=pltpu.VMEM), pl.BlockSpec(memory_space=pltpu.SMEM)
    both = exchange(send)
    last = out_gain[:, None], out_bias[:, None], out_weight
    late = call(
        gate_kernel, [shape((count, WIDTH), F32)] + [shape(value.shape, value.dtype) for value in last], name="gate"
    )(normed, gate_weight, *last)
    late, both = lax.optimization_barrier((late, both))
    keep, away = pl.pallas_call(
        right_kernel,
        out_shape=(shape((JSPAN, SIDE), BF16),) * 2,
        in_specs=[vmem, smem],
        compiler_params=pltpu.CompilerParams(vmem_limit_bytes=16 * 2**20),
        name="right",
    )(both, core)
    mirror = lax.ppermute(keep, AXES, swap(True, False))
    cross = lax.ppermute(away, AXES, swap(True, True))
    bundle = call(left_kernel, shape((SIDE + JSPAN, SIDE), BF16), name="left")(both, away)
    bundle_core = lax.ppermute(bundle, AXES, swap(False, True))
    own = pl.pallas_call(
        own_kernel,
        out_shape=shape((SIDE // LANES, SIDE, LANES), F32),
        in_specs=[vmem] * 3 + [smem],
        compiler_params=pltpu.CompilerParams(vmem_limit_bytes=16 * 2**20),
        cost_estimate=pl.CostEstimate(flops=SIDE * SIDE * SIDE * 2 * COST_SCALE, bytes_accessed=0, transcendentals=0),
        name="own",
    )(bundle, keep, mirror, side)
    combined = pl.pallas_call(
        contract_kernel,
        out_shape=shape((RPOS * QPOS, 2, SPAN + ROWS), BF16),
        in_specs=[vmem] * 3 + [smem],
        scratch_shapes=[pltpu.VMEM((SIDE // LANES, SIDE, LANES), F32)],
        compiler_params=pltpu.CompilerParams(vmem_limit_bytes=16 * 2**20),
        name="contract",
    )(bundle_core, cross, own, side)
    combined = exchange(combined)
    update = call(
        update_kernel,
        shape((count, WIDTH), BF16),
        (pltpu.VMEM((pl.cdiv(SPAN + ROWS, LANES), 2 * WIDTH, LANES), F32), pltpu.VMEM((count, WIDTH), F32)),
        "update",
    )(combined, *late)
    return update.reshape(ROWS, COLS, WIDTH)


def solution(mesh):
    return jax.shard_map(
        per_device,
        mesh=mesh,
        in_specs=(P("row", "col", None), P("row", "col"), P(), P(), P(), P(), P(), P(), P()),
        out_specs=P("row", "col", None),
        check_vma=False,
    )
```

```python
import functools

import jax
import jax.numpy as jnp
from jax import lax
from jax.experimental import pallas as pl
from jax.experimental.pallas import tpu as pltpu
from jax.sharding import PartitionSpec as P

BF16 = jnp.bfloat16
F32 = jnp.float32
AXES = ("row", "col")
ROWS, COLS, WIDTH = 48, 24, 128
COST_SCALE = 100
HALF = COLS // 2
SPAN = HALF * ROWS
RPOS, QPOS = 8, 16
LANES = 128
SIDE = RPOS * ROWS
JSPAN = RPOS * COLS


def sigmoid(x):
    return 0.5 * jnp.tanh(0.5 * x) + 0.5


def device(z_hi, x, z_lo, y, core):
    return (z_hi * 4 + x) * 32 + z_lo * 16 + y * 2 + core


def x_of(side, x_low):
    return x_low if side == 0 else 3 - x_low


def lead(items, start):
    return items[start:] + items[:start]


ROW_ORDER = lead([(zh, xl) for zh in range(4) for xl in range(2)], 4)
COL_ORDER = lead([(zl, y) for zl in range(2) for y in range(8)], 12)


def positions():
    return [(zh, xl, zl, y) for zh, xl in ROW_ORDER for zl, y in COL_ORDER]


def column_position(z_hi, x):
    row = z_hi * 4 + x
    return COL_ORDER.index((row // 8, row % 8))


def channel_groups():
    return [
        [device(zh, x_of(side, xl), zl, y, core) for zh, xl, zl, y in positions()]
        for side in range(2)
        for core in range(2)
    ]


def swap(mirror, core):
    return [
        (device(zh, x, zl, y, c), device(zh, 3 - x if mirror else x, zl, y, 1 - c if core else c))
        for zh in range(4)
        for x in range(4)
        for zl in range(2)
        for y in range(8)
        for c in range(2)
    ]


def dot(a, b, dims):
    return lax.dot_general(a, b, (dims, ((), ())), preferred_element_type=F32)


def call(kernel, out_shape, scratch=(), name=None):
    return pl.pallas_call(
        kernel,
        out_shape=out_shape,
        scratch_shapes=list(scratch),
        compiler_params=pltpu.CompilerParams(vmem_limit_bytes=16 * 2**20),
        name=name,
    )


def factors_kernel(*refs):
    given, (send_ref, normed_ref), held = refs[:5], refs[5:7], refs[7:12]
    tokens, pairs, sems = refs[12:]
    copies = [pltpu.make_async_copy(src, dst, sems.at[n]) for n, (src, dst) in enumerate(zip(given, held))]
    for copy in copies:
        copy.start()
    for copy in copies:
        copy.wait()
    x_ref, mask_ref, gain_ref, bias_ref, w_ref = held
    tokens[...] = x_ref[...].astype(F32)
    values = jnp.concatenate([tokens[pl.ds(k, ROWS, stride=COLS), :] for k in range(COLS)], axis=0)
    mean = jnp.mean(values, axis=-1, keepdims=True)
    centred = values - mean
    var = jnp.mean(centred * centred, axis=-1, keepdims=True)
    normed = (centred * lax.rsqrt(var + 1e-05) * gain_ref[...] + bias_ref[...]).astype(BF16)
    normed_ref[...] = normed
    token = lax.broadcasted_iota(jnp.int32, (ROWS, ROWS * COLS), 1)
    spread = (lax.rem(token, ROWS) == lax.broadcasted_iota(jnp.int32, token.shape, 0)).astype(BF16)
    every = dot(mask_ref[...].astype(F32).astype(BF16), spread, ((1,), (0,)))
    token = lax.broadcasted_iota(jnp.int32, every.shape, 1)
    first = lax.broadcasted_iota(jnp.int32, every.shape, 0) * ROWS
    mask = jnp.sum(jnp.where((token >= first) & (token < first + ROWS), every, 0.0), axis=0, keepdims=True)
    weight = w_ref[...].T
    for half in range(2):
        part = normed[half * SPAN : (half + 1) * SPAN]
        part_mask = mask[:, half * SPAN : (half + 1) * SPAN]
        sides = []
        for side in range(2):
            hidden = dot(weight[side * 2 * WIDTH : (side + 1) * 2 * WIDTH], part, ((1,), (1,)))
            sides.append(sigmoid(hidden[WIDTH:]) * hidden[:WIDTH] * part_mask)
        both = jnp.concatenate(sides, axis=1)
        for t in range(2 * SPAN // LANES):
            pairs[t, pl.ds(half, WIDTH, stride=2), :] = both[:, t * LANES : (t + 1) * LANES]
    for t in range(2 * SPAN // LANES):
        send_ref[:, :, t * LANES : (t + 1) * LANES] = pairs[t].astype(BF16).reshape(WIDTH, 2, LANES)


def gate_kernel(normed_ref, w_ref, *rest_refs):
    *from_refs, gate_ref, gain_ref, bias_ref, out_w_ref = rest_refs
    gate_ref[...] = sigmoid(dot(normed_ref[...], w_ref[...], ((1,), (0,))))
    for source, target in zip(from_refs, (gain_ref, bias_ref, out_w_ref)):
        target[...] = source[...]


def right_kernel(x_ref, core_ref, keep_ref, send_ref):
    x = x_ref[...].reshape(RPOS * QPOS * 2, 2 * SPAN)[:, SPAN:]
    core = core_ref[0]
    rows = 2 * QPOS
    for k in range(HALF // 2):
        blocks = [
            jnp.concatenate(
                [
                    x[rp * rows : (rp + 1) * rows, (h * 6 + k) * ROWS + b * COLS : (h * 6 + k) * ROWS + (b + 1) * COLS]
                    for h in range(2)
                    for rp in range(RPOS)
                ],
                axis=1,
            )
            for b in range(2)
        ]
        keep_ref[k * rows : (k + 1) * rows, :] = jnp.where(core == 0, blocks[0], blocks[1])
        send_ref[k * rows : (k + 1) * rows, :] = jnp.where(core == 0, blocks[1], blocks[0])


def left_kernel(x_ref, away_ref, out_ref):
    x = x_ref[...].reshape(RPOS * QPOS * 2, 2 * SPAN)[:, :SPAN]
    rows = 2 * QPOS
    for k in range(HALF):
        out_ref[k * rows : (k + 1) * rows, :] = jnp.concatenate(
            [x[rp * rows : (rp + 1) * rows, k * ROWS : (k + 1) * ROWS] for rp in range(RPOS)], axis=1
        )
    out_ref[SIDE:, :] = away_ref[...]


def add_products(left, here, mirror, side, total, earlier=None):
    for at, right in ((side, here), (1 - side, mirror)):
        part = jnp.zeros((JSPAN, SIDE), F32)
        for h in range(2):
            part += dot(right[:, h * JSPAN : (h + 1) * JSPAN], left[h * JSPAN : (h + 1) * JSPAN], ((0,), (0,)))
        for rp, (z_hi, x_low) in enumerate(ROW_ORDER):
            places = [column_position(z_hi, x_of(s, x_low)) * COLS for s in range(2)]
            rows = pl.ds(pl.multiple_of(jnp.where(at == 0, places[0], places[1]), 8), COLS)
            for t in range(SIDE // LANES):
                piece = part[rp * COLS : (rp + 1) * COLS, t * LANES : (t + 1) * LANES]
                total[t, rows, :] = piece if earlier is None else piece + earlier[t, rows, :]


def own_kernel(bundle_ref, keep_ref, mirror_ref, side_ref, total_ref):
    add_products(bundle_ref[:SIDE], keep_ref[...], mirror_ref[...], side_ref[0], total_ref)


def contract_kernel(bundle_ref, cross_ref, own_ref, side_ref, send_ref, total):
    add_products(bundle_ref[:SIDE], bundle_ref[SIDE:], cross_ref[...], side_ref[0], total, own_ref)
    rows = 2 * QPOS
    blocks = [
        jnp.concatenate([total[t, pl.ds(j, rows, stride=HALF), :] for t in range(SIDE // LANES)], axis=1)
        for j in range(HALF)
    ]
    base = (functools.reduce(jnp.add, blocks) * (1.0 / HALF)).astype(BF16).astype(F32)
    blocks = [block - base for block in blocks] + [base]
    for rp in range(RPOS):
        piece = jnp.concatenate([block[:, rp * ROWS : (rp + 1) * ROWS] for block in blocks], axis=1)
        send_ref[rp * QPOS : (rp + 1) * QPOS] = piece.astype(BF16).reshape(QPOS, 2, SPAN + ROWS)


def update_kernel(x_ref, gate_ref, gain_ref, bias_ref, w_ref, out_ref, pairs, tokens):
    arrived = x_ref[...].reshape(2 * WIDTH, SPAN + ROWS).astype(F32)
    tiles = pl.cdiv(SPAN + ROWS, LANES)
    for t in range(tiles):
        tile = arrived[:, t * LANES : (t + 1) * LANES]
        pairs[t, :, : tile.shape[1]] = tile
    for half in range(2):
        values = [pairs[t, pl.ds(half, WIDTH, stride=2), :] for t in range(tiles)]
        values = jnp.concatenate(values, axis=1)
        base = values[:, SPAN : SPAN + ROWS]
        values = values[:, :SPAN] + jnp.concatenate([base] * HALF, axis=1)
        mean = jnp.mean(values, axis=0, keepdims=True)
        centred = values - mean
        var = jnp.mean(centred * centred, axis=0, keepdims=True)
        onorm = (centred * lax.rsqrt(var + 1e-05) * gain_ref[...] + bias_ref[...]).astype(BF16)
        update = dot(onorm, w_ref[...], ((0,), (0,))) * gate_ref[half * SPAN : (half + 1) * SPAN]
        for j in range(HALF):
            tokens[pl.ds(half * HALF + j, ROWS, stride=COLS), :] = update[j * ROWS : (j + 1) * ROWS]
    out_ref[...] = tokens[...].astype(BF16)


def per_device(
    pair, pair_mask, in_gain, in_bias, proj_weight, gate_weight, out_gain, out_bias, out_weight
):
    shape = jax.ShapeDtypeStruct
    count = ROWS * COLS
    given = pair.reshape(count, WIDTH), pair_mask.T, in_gain[None], in_bias[None], proj_weight
    send, normed = pl.pallas_call(
        factors_kernel,
        out_shape=(shape((WIDTH, 2, 2 * SPAN), BF16), shape((count, WIDTH), BF16)),
        in_specs=[pl.BlockSpec(memory_space=pl.ANY)] * 5,
        scratch_shapes=[pltpu.VMEM(value.shape, value.dtype) for value in given]
        + [
            pltpu.VMEM((count, WIDTH), F32),
            pltpu.VMEM((2 * SPAN // LANES, 2 * WIDTH, LANES), F32),
            pltpu.SemaphoreType.DMA((5,)),
        ],
        compiler_params=pltpu.CompilerParams(vmem_limit_bytes=56 * 2**20),
        name="factors",
    )(*given)
    exchange = functools.partial(
        lax.all_to_all, axis_name=AXES, split_axis=0, concat_axis=0, axis_index_groups=channel_groups(), tiled=True
    )
    core = lax.rem(lax.axis_index("col"), 2).astype(jnp.int32).reshape(1)
    side = (lax.rem(lax.axis_index("row"), 4) // 2).astype(jnp.int32).reshape(1)
    vmem, smem = pl.BlockSpec(memory_space=pltpu.VMEM), pl.BlockSpec(memory_space=pltpu.SMEM)
    both = exchange(send)
    last = out_gain[:, None], out_bias[:, None], out_weight
    late = call(
        gate_kernel, [shape((count, WIDTH), F32)] + [shape(value.shape, value.dtype) for value in last], name="gate"
    )(normed, gate_weight, *last)
    keep, away = pl.pallas_call(
        right_kernel,
        out_shape=(shape((JSPAN, SIDE), BF16),) * 2,
        in_specs=[vmem, smem],
        compiler_params=pltpu.CompilerParams(vmem_limit_bytes=16 * 2**20),
        name="right",
    )(both, core)
    late, keep = lax.optimization_barrier((late, keep))
    mirror = lax.ppermute(keep, AXES, swap(True, False))
    cross = lax.ppermute(away, AXES, swap(True, True))
    bundle = call(left_kernel, shape((SIDE + JSPAN, SIDE), BF16), name="left")(both, away)
    bundle_core = lax.ppermute(bundle, AXES, swap(False, True))
    own = pl.pallas_call(
        own_kernel,
        out_shape=shape((SIDE // LANES, SIDE, LANES), F32),
        in_specs=[vmem] * 3 + [smem],
        compiler_params=pltpu.CompilerParams(vmem_limit_bytes=16 * 2**20),
        cost_estimate=pl.CostEstimate(flops=SIDE * SIDE * SIDE * 2 * COST_SCALE, bytes_accessed=0, transcendentals=0),
        name="own",
    )(bundle, keep, mirror, side)
    combined = pl.pallas_call(
        contract_kernel,
        out_shape=shape((RPOS * QPOS, 2, SPAN + ROWS), BF16),
        in_specs=[vmem] * 3 + [smem],
        scratch_shapes=[pltpu.VMEM((SIDE // LANES, SIDE, LANES), F32)],
        compiler_params=pltpu.CompilerParams(vmem_limit_bytes=16 * 2**20),
        name="contract",
    )(bundle_core, cross, own, side)
    combined = exchange(combined)
    update = call(
        update_kernel,
        shape((count, WIDTH), BF16),
        (pltpu.VMEM((pl.cdiv(SPAN + ROWS, LANES), 2 * WIDTH, LANES), F32), pltpu.VMEM((count, WIDTH), F32)),
        "update",
    )(combined, *late)
    return update.reshape(ROWS, COLS, WIDTH)


def solution(mesh):
    return jax.shard_map(
        per_device,
        mesh=mesh,
        in_specs=(P("row", "col", None), P("row", "col"), P(), P(), P(), P(), P(), P(), P()),
        out_specs=P("row", "col", None),
        check_vma=False,
    )
```

```python
import functools

import jax
import jax.numpy as jnp
from jax import lax
from jax.experimental import pallas as pl
from jax.experimental.pallas import tpu as pltpu
from jax.sharding import PartitionSpec as P

BF16 = jnp.bfloat16
F32 = jnp.float32
AXES = ("row", "col")
ROWS, COLS, WIDTH = 48, 24, 128
COST_SCALE = 100
HALF = COLS // 2
SPAN = HALF * ROWS
RPOS, QPOS = 8, 16
LANES = 128
SIDE = RPOS * ROWS
JSPAN = RPOS * COLS


def sigmoid(x):
    return 0.5 * jnp.tanh(0.5 * x) + 0.5


def device(z_hi, x, z_lo, y, core):
    return (z_hi * 4 + x) * 32 + z_lo * 16 + y * 2 + core


def x_of(side, x_low):
    return x_low if side == 0 else 3 - x_low


def ring(a, b):
    return min((a - b) % 8, (b - a) % 8)


def from_far(items, first, distance):
    return [first] + sorted([item for item in items if item != first], key=lambda item: -distance(item))


ROW_ORDER = from_far(
    [(zh, xl) for zh in range(4) for xl in range(2)], (2, 0), lambda place: ring(2 * place[0], 4) + place[1]
)
COL_ORDER = from_far(
    [(zl, y) for zl in range(2) for y in range(8)], (1, 4), lambda place: ring(place[1], 4) + 1 - place[0]
)


def positions():
    return [(zh, xl, zl, y) for zh, xl in ROW_ORDER for zl, y in COL_ORDER]


def column_position(z_hi, x):
    row = z_hi * 4 + x
    return COL_ORDER.index((row // 8, row % 8))


def channel_groups():
    return [
        [device(zh, x_of(side, xl), zl, y, core) for zh, xl, zl, y in positions()]
        for side in range(2)
        for core in range(2)
    ]


def swap(mirror, core):
    return [
        (device(zh, x, zl, y, c), device(zh, 3 - x if mirror else x, zl, y, 1 - c if core else c))
        for zh in range(4)
        for x in range(4)
        for zl in range(2)
        for y in range(8)
        for c in range(2)
    ]


def dot(a, b, dims):
    return lax.dot_general(a, b, (dims, ((), ())), preferred_element_type=F32)


def call(kernel, out_shape, scratch=(), name=None):
    return pl.pallas_call(
        kernel,
        out_shape=out_shape,
        scratch_shapes=list(scratch),
        compiler_params=pltpu.CompilerParams(vmem_limit_bytes=16 * 2**20),
        name=name,
    )


def factors_kernel(*refs):
    given, (send_ref, normed_ref), held = refs[:5], refs[5:7], refs[7:12]
    tokens, pairs, sems = refs[12:]
    copies = [pltpu.make_async_copy(src, dst, sems.at[n]) for n, (src, dst) in enumerate(zip(given, held))]
    for copy in copies:
        copy.start()
    for copy in copies:
        copy.wait()
    x_ref, mask_ref, gain_ref, bias_ref, w_ref = held
    tokens[...] = x_ref[...].astype(F32)
    values = jnp.concatenate([tokens[pl.ds(k, ROWS, stride=COLS), :] for k in range(COLS)], axis=0)
    mean = jnp.mean(values, axis=-1, keepdims=True)
    centred = values - mean
    var = jnp.mean(centred * centred, axis=-1, keepdims=True)
    normed = (centred * lax.rsqrt(var + 1e-05) * gain_ref[...] + bias_ref[...]).astype(BF16)
    normed_ref[...] = normed
    token = lax.broadcasted_iota(jnp.int32, (ROWS, ROWS * COLS), 1)
    spread = (lax.rem(token, ROWS) == lax.broadcasted_iota(jnp.int32, token.shape, 0)).astype(BF16)
    every = dot(mask_ref[...].astype(F32).astype(BF16), spread, ((1,), (0,)))
    token = lax.broadcasted_iota(jnp.int32, every.shape, 1)
    first = lax.broadcasted_iota(jnp.int32, every.shape, 0) * ROWS
    mask = jnp.sum(jnp.where((token >= first) & (token < first + ROWS), every, 0.0), axis=0, keepdims=True)
    weight = w_ref[...].T
    for half in range(2):
        part = normed[half * SPAN : (half + 1) * SPAN]
        part_mask = mask[:, half * SPAN : (half + 1) * SPAN]
        sides = []
        for side in range(2):
            hidden = dot(weight[side * 2 * WIDTH : (side + 1) * 2 * WIDTH], part, ((1,), (1,)))
            sides.append(sigmoid(hidden[WIDTH:]) * hidden[:WIDTH] * part_mask)
        both = jnp.concatenate(sides, axis=1)
        for t in range(2 * SPAN // LANES):
            pairs[t, pl.ds(half, WIDTH, stride=2), :] = both[:, t * LANES : (t + 1) * LANES]
    for t in range(2 * SPAN // LANES):
        send_ref[:, :, t * LANES : (t + 1) * LANES] = pairs[t].astype(BF16).reshape(WIDTH, 2, LANES)


def gate_kernel(normed_ref, w_ref, *rest_refs):
    *from_refs, gate_ref, gain_ref, bias_ref, out_w_ref = rest_refs
    gate_ref[...] = sigmoid(dot(normed_ref[...], w_ref[...], ((1,), (0,))))
    for source, target in zip(from_refs, (gain_ref, bias_ref, out_w_ref)):
        target[...] = source[...]


def right_kernel(x_ref, core_ref, keep_ref, send_ref):
    x = x_ref[...].reshape(RPOS * QPOS * 2, 2 * SPAN)[:, SPAN:]
    core = core_ref[0]
    rows = 2 * QPOS
    for k in range(HALF // 2):
        blocks = [
            jnp.concatenate(
                [
                    x[rp * rows : (rp + 1) * rows, (h * 6 + k) * ROWS + b * COLS : (h * 6 + k) * ROWS + (b + 1) * COLS]
                    for h in range(2)
                    for rp in range(RPOS)
                ],
                axis=1,
            )
            for b in range(2)
        ]
        keep_ref[k * rows : (k + 1) * rows, :] = jnp.where(core == 0, blocks[0], blocks[1])
        send_ref[k * rows : (k + 1) * rows, :] = jnp.where(core == 0, blocks[1], blocks[0])


def left_kernel(x_ref, away_ref, out_ref):
    x = x_ref[...].reshape(RPOS * QPOS * 2, 2 * SPAN)[:, :SPAN]
    rows = 2 * QPOS
    for k in range(HALF):
        out_ref[k * rows : (k + 1) * rows, :] = jnp.concatenate(
            [x[rp * rows : (rp + 1) * rows, k * ROWS : (k + 1) * ROWS] for rp in range(RPOS)], axis=1
        )
    out_ref[SIDE:, :] = away_ref[...]


def add_products(left, here, mirror, side, total, earlier=None):
    for at, right in ((side, here), (1 - side, mirror)):
        part = jnp.zeros((JSPAN, SIDE), F32)
        for h in range(2):
            part += dot(right[:, h * JSPAN : (h + 1) * JSPAN], left[h * JSPAN : (h + 1) * JSPAN], ((0,), (0,)))
        for rp, (z_hi, x_low) in enumerate(ROW_ORDER):
            places = [column_position(z_hi, x_of(s, x_low)) * COLS for s in range(2)]
            rows = pl.ds(pl.multiple_of(jnp.where(at == 0, places[0], places[1]), 8), COLS)
            for t in range(SIDE // LANES):
                piece = part[rp * COLS : (rp + 1) * COLS, t * LANES : (t + 1) * LANES]
                total[t, rows, :] = piece if earlier is None else piece + earlier[t, rows, :]


def own_kernel(bundle_ref, keep_ref, mirror_ref, side_ref, total_ref):
    add_products(bundle_ref[:SIDE], keep_ref[...], mirror_ref[...], side_ref[0], total_ref)


def contract_kernel(bundle_ref, cross_ref, own_ref, side_ref, send_ref, total):
    add_products(bundle_ref[:SIDE], bundle_ref[SIDE:], cross_ref[...], side_ref[0], total, own_ref)
    rows = 2 * QPOS
    blocks = [
        jnp.concatenate([total[t, pl.ds(j, rows, stride=HALF), :] for t in range(SIDE // LANES)], axis=1)
        for j in range(HALF)
    ]
    base = (functools.reduce(jnp.add, blocks) * (1.0 / HALF)).astype(BF16).astype(F32)
    blocks = [block - base for block in blocks] + [base]
    for rp in range(RPOS):
        piece = jnp.concatenate([block[:, rp * ROWS : (rp + 1) * ROWS] for block in blocks], axis=1)
        send_ref[rp * QPOS : (rp + 1) * QPOS] = piece.astype(BF16).reshape(QPOS, 2, SPAN + ROWS)


def update_kernel(x_ref, gate_ref, gain_ref, bias_ref, w_ref, out_ref, pairs, tokens):
    arrived = x_ref[...].reshape(2 * WIDTH, SPAN + ROWS).astype(F32)
    tiles = pl.cdiv(SPAN + ROWS, LANES)
    for t in range(tiles):
        tile = arrived[:, t * LANES : (t + 1) * LANES]
        pairs[t, :, : tile.shape[1]] = tile
    for half in range(2):
        values = [pairs[t, pl.ds(half, WIDTH, stride=2), :] for t in range(tiles)]
        values = jnp.concatenate(values, axis=1)
        base = values[:, SPAN : SPAN + ROWS]
        values = values[:, :SPAN] + jnp.concatenate([base] * HALF, axis=1)
        mean = jnp.mean(values, axis=0, keepdims=True)
        centred = values - mean
        var = jnp.mean(centred * centred, axis=0, keepdims=True)
        onorm = (centred * lax.rsqrt(var + 1e-05) * gain_ref[...] + bias_ref[...]).astype(BF16)
        update = dot(onorm, w_ref[...], ((0,), (0,))) * gate_ref[half * SPAN : (half + 1) * SPAN]
        for j in range(HALF):
            tokens[pl.ds(half * HALF + j, ROWS, stride=COLS), :] = update[j * ROWS : (j + 1) * ROWS]
    out_ref[...] = tokens[...].astype(BF16)


def per_device(
    pair, pair_mask, in_gain, in_bias, proj_weight, gate_weight, out_gain, out_bias, out_weight
):
    shape = jax.ShapeDtypeStruct
    count = ROWS * COLS
    given = pair.reshape(count, WIDTH), pair_mask.T, in_gain[None], in_bias[None], proj_weight
    send, normed = pl.pallas_call(
        factors_kernel,
        out_shape=(shape((WIDTH, 2, 2 * SPAN), BF16), shape((count, WIDTH), BF16)),
        in_specs=[pl.BlockSpec(memory_space=pl.ANY)] * 5,
        scratch_shapes=[pltpu.VMEM(value.shape, value.dtype) for value in given]
        + [
            pltpu.VMEM((count, WIDTH), F32),
            pltpu.VMEM((2 * SPAN // LANES, 2 * WIDTH, LANES), F32),
            pltpu.SemaphoreType.DMA((5,)),
        ],
        compiler_params=pltpu.CompilerParams(vmem_limit_bytes=56 * 2**20),
        name="factors",
    )(*given)
    exchange = functools.partial(
        lax.all_to_all, axis_name=AXES, split_axis=0, concat_axis=0, axis_index_groups=channel_groups(), tiled=True
    )
    core = lax.rem(lax.axis_index("col"), 2).astype(jnp.int32).reshape(1)
    side = (lax.rem(lax.axis_index("row"), 4) // 2).astype(jnp.int32).reshape(1)
    vmem, smem = pl.BlockSpec(memory_space=pltpu.VMEM), pl.BlockSpec(memory_space=pltpu.SMEM)
    both = exchange(send)
    last = out_gain[:, None], out_bias[:, None], out_weight
    late = call(
        gate_kernel, [shape((count, WIDTH), F32)] + [shape(value.shape, value.dtype) for value in last], name="gate"
    )(normed, gate_weight, *last)
    keep, away = pl.pallas_call(
        right_kernel,
        out_shape=(shape((JSPAN, SIDE), BF16),) * 2,
        in_specs=[vmem, smem],
        compiler_params=pltpu.CompilerParams(vmem_limit_bytes=16 * 2**20),
        name="right",
    )(both, core)
    late, keep = lax.optimization_barrier((late, keep))
    mirror = lax.ppermute(keep, AXES, swap(True, False))
    cross = lax.ppermute(away, AXES, swap(True, True))
    bundle = call(left_kernel, shape((SIDE + JSPAN, SIDE), BF16), name="left")(both, away)
    bundle_core = lax.ppermute(bundle, AXES, swap(False, True))
    own = pl.pallas_call(
        own_kernel,
        out_shape=shape((SIDE // LANES, SIDE, LANES), F32),
        in_specs=[vmem] * 3 + [smem],
        compiler_params=pltpu.CompilerParams(vmem_limit_bytes=16 * 2**20),
        cost_estimate=pl.CostEstimate(flops=SIDE * SIDE * SIDE * 2 * COST_SCALE, bytes_accessed=0, transcendentals=0),
        name="own",
    )(bundle, keep, mirror, side)
    combined = pl.pallas_call(
        contract_kernel,
        out_shape=shape((RPOS * QPOS, 2, SPAN + ROWS), BF16),
        in_specs=[vmem] * 3 + [smem],
        scratch_shapes=[pltpu.VMEM((SIDE // LANES, SIDE, LANES), F32)],
        compiler_params=pltpu.CompilerParams(vmem_limit_bytes=16 * 2**20),
        name="contract",
    )(bundle_core, cross, own, side)
    combined = exchange(combined)
    update = call(
        update_kernel,
        shape((count, WIDTH), BF16),
        (pltpu.VMEM((pl.cdiv(SPAN + ROWS, LANES), 2 * WIDTH, LANES), F32), pltpu.VMEM((count, WIDTH), F32)),
        "update",
    )(combined, *late)
    return update.reshape(ROWS, COLS, WIDTH)


def solution(mesh):
    return jax.shard_map(
        per_device,
        mesh=mesh,
        in_specs=(P("row", "col", None), P("row", "col"), P(), P(), P(), P(), P(), P(), P()),
        out_specs=P("row", "col", None),
        check_vma=False,
    )
```

```python
import functools

import jax
import jax.numpy as jnp
from jax import lax
from jax.experimental import pallas as pl
from jax.experimental.pallas import tpu as pltpu
from jax.sharding import PartitionSpec as P

BF16 = jnp.bfloat16
F32 = jnp.float32
AXES = ("row", "col")
ROWS, COLS, WIDTH = 48, 24, 128
COST_SCALE = 100
HALF = COLS // 2
SPAN = HALF * ROWS
RPOS, QPOS = 8, 16
LANES = 128
SIDE = RPOS * ROWS
JSPAN = RPOS * COLS


def sigmoid(x):
    return 0.5 * jnp.tanh(0.5 * x) + 0.5


def device(z_hi, x, z_lo, y, core):
    return (z_hi * 4 + x) * 32 + z_lo * 16 + y * 2 + core


def x_of(side, x_low):
    return x_low if side == 0 else 3 - x_low


def ring(a, b):
    return min((a - b) % 8, (b - a) % 8)


def from_far(items, first, distance):
    return [first] + sorted([item for item in items if item != first], key=lambda item: -distance(item))


ROW_ORDER = from_far(
    [(zh, xl) for zh in range(4) for xl in range(2)], (2, 0), lambda place: (ring(2 * place[0], 5) + ring(2 * place[0] + 1, 5)) / 2 + place[1]
)
COL_ORDER = from_far(
    [(zl, y) for zl in range(2) for y in range(8)], (1, 4), lambda place: ring(place[1], 4) + 1 - place[0]
)


def positions():
    return [(zh, xl, zl, y) for zh, xl in ROW_ORDER for zl, y in COL_ORDER]


def column_position(z_hi, x):
    row = z_hi * 4 + x
    return COL_ORDER.index((row // 8, row % 8))


def channel_groups():
    return [
        [device(zh, x_of(side, xl), zl, y, core) for zh, xl, zl, y in positions()]
        for side in range(2)
        for core in range(2)
    ]


def swap(mirror, core):
    return [
        (device(zh, x, zl, y, c), device(zh, 3 - x if mirror else x, zl, y, 1 - c if core else c))
        for zh in range(4)
        for x in range(4)
        for zl in range(2)
        for y in range(8)
        for c in range(2)
    ]


def dot(a, b, dims):
    return lax.dot_general(a, b, (dims, ((), ())), preferred_element_type=F32)


def call(kernel, out_shape, scratch=(), name=None):
    return pl.pallas_call(
        kernel,
        out_shape=out_shape,
        scratch_shapes=list(scratch),
        compiler_params=pltpu.CompilerParams(vmem_limit_bytes=16 * 2**20),
        name=name,
    )


def factors_kernel(*refs):
    given, (send_ref, normed_ref), held = refs[:5], refs[5:7], refs[7:12]
    tokens, pairs, sems = refs[12:]
    copies = [pltpu.make_async_copy(src, dst, sems.at[n]) for n, (src, dst) in enumerate(zip(given, held))]
    for copy in copies:
        copy.start()
    for copy in copies:
        copy.wait()
    x_ref, mask_ref, gain_ref, bias_ref, w_ref = held
    tokens[...] = x_ref[...].astype(F32)
    values = jnp.concatenate([tokens[pl.ds(k, ROWS, stride=COLS), :] for k in range(COLS)], axis=0)
    mean = jnp.mean(values, axis=-1, keepdims=True)
    centred = values - mean
    var = jnp.mean(centred * centred, axis=-1, keepdims=True)
    normed = (centred * lax.rsqrt(var + 1e-05) * gain_ref[...] + bias_ref[...]).astype(BF16)
    normed_ref[...] = normed
    token = lax.broadcasted_iota(jnp.int32, (ROWS, ROWS * COLS), 1)
    spread = (lax.rem(token, ROWS) == lax.broadcasted_iota(jnp.int32, token.shape, 0)).astype(BF16)
    every = dot(mask_ref[...].astype(F32).astype(BF16), spread, ((1,), (0,)))
    token = lax.broadcasted_iota(jnp.int32, every.shape, 1)
    first = lax.broadcasted_iota(jnp.int32, every.shape, 0) * ROWS
    mask = jnp.sum(jnp.where((token >= first) & (token < first + ROWS), every, 0.0), axis=0, keepdims=True)
    weight = w_ref[...].T
    for half in range(2):
        part = normed[half * SPAN : (half + 1) * SPAN]
        part_mask = mask[:, half * SPAN : (half + 1) * SPAN]
        sides = []
        for side in range(2):
            hidden = dot(weight[side * 2 * WIDTH : (side + 1) * 2 * WIDTH], part, ((1,), (1,)))
            sides.append(sigmoid(hidden[WIDTH:]) * hidden[:WIDTH] * part_mask)
        both = jnp.concatenate(sides, axis=1)
        for t in range(2 * SPAN // LANES):
            pairs[t, pl.ds(half, WIDTH, stride=2), :] = both[:, t * LANES : (t + 1) * LANES]
    for t in range(2 * SPAN // LANES):
        send_ref[:, :, t * LANES : (t + 1) * LANES] = pairs[t].astype(BF16).reshape(WIDTH, 2, LANES)


def gate_kernel(normed_ref, w_ref, *rest_refs):
    *from_refs, gate_ref, gain_ref, bias_ref, out_w_ref = rest_refs
    gate_ref[...] = sigmoid(dot(normed_ref[...], w_ref[...], ((1,), (0,))))
    for source, target in zip(from_refs, (gain_ref, bias_ref, out_w_ref)):
        target[...] = source[...]


def right_kernel(x_ref, core_ref, keep_ref, send_ref):
    x = x_ref[...].reshape(RPOS * QPOS * 2, 2 * SPAN)[:, SPAN:]
    core = core_ref[0]
    rows = 2 * QPOS
    for k in range(HALF // 2):
        blocks = [
            jnp.concatenate(
                [
                    x[rp * rows : (rp + 1) * rows, (h * 6 + k) * ROWS + b * COLS : (h * 6 + k) * ROWS + (b + 1) * COLS]
                    for h in range(2)
                    for rp in range(RPOS)
                ],
                axis=1,
            )
            for b in range(2)
        ]
        keep_ref[k * rows : (k + 1) * rows, :] = jnp.where(core == 0, blocks[0], blocks[1])
        send_ref[k * rows : (k + 1) * rows, :] = jnp.where(core == 0, blocks[1], blocks[0])


def left_kernel(x_ref, away_ref, out_ref):
    x = x_ref[...].reshape(RPOS * QPOS * 2, 2 * SPAN)[:, :SPAN]
    rows = 2 * QPOS
    for k in range(HALF):
        out_ref[k * rows : (k + 1) * rows, :] = jnp.concatenate(
            [x[rp * rows : (rp + 1) * rows, k * ROWS : (k + 1) * ROWS] for rp in range(RPOS)], axis=1
        )
    out_ref[SIDE:, :] = away_ref[...]


def add_products(left, here, mirror, side, total, earlier=None):
    for at, right in ((side, here), (1 - side, mirror)):
        part = jnp.zeros((JSPAN, SIDE), F32)
        for h in range(2):
            part += dot(right[:, h * JSPAN : (h + 1) * JSPAN], left[h * JSPAN : (h + 1) * JSPAN], ((0,), (0,)))
        for rp, (z_hi, x_low) in enumerate(ROW_ORDER):
            places = [column_position(z_hi, x_of(s, x_low)) * COLS for s in range(2)]
            rows = pl.ds(pl.multiple_of(jnp.where(at == 0, places[0], places[1]), 8), COLS)
            for t in range(SIDE // LANES):
                piece = part[rp * COLS : (rp + 1) * COLS, t * LANES : (t + 1) * LANES]
                total[t, rows, :] = piece if earlier is None else piece + earlier[t, rows, :]


def own_kernel(bundle_ref, keep_ref, mirror_ref, side_ref, total_ref):
    add_products(bundle_ref[:SIDE], keep_ref[...], mirror_ref[...], side_ref[0], total_ref)


def contract_kernel(bundle_ref, cross_ref, own_ref, side_ref, send_ref, total):
    add_products(bundle_ref[:SIDE], bundle_ref[SIDE:], cross_ref[...], side_ref[0], total, own_ref)
    rows = 2 * QPOS
    blocks = [
        jnp.concatenate([total[t, pl.ds(j, rows, stride=HALF), :] for t in range(SIDE // LANES)], axis=1)
        for j in range(HALF)
    ]
    base = (functools.reduce(jnp.add, blocks) * (1.0 / HALF)).astype(BF16).astype(F32)
    blocks = [block - base for block in blocks] + [base]
    for rp in range(RPOS):
        piece = jnp.concatenate([block[:, rp * ROWS : (rp + 1) * ROWS] for block in blocks], axis=1)
        send_ref[rp * QPOS : (rp + 1) * QPOS] = piece.astype(BF16).reshape(QPOS, 2, SPAN + ROWS)


def update_kernel(x_ref, gate_ref, gain_ref, bias_ref, w_ref, out_ref, pairs, tokens):
    arrived = x_ref[...].reshape(2 * WIDTH, SPAN + ROWS).astype(F32)
    tiles = pl.cdiv(SPAN + ROWS, LANES)
    for t in range(tiles):
        tile = arrived[:, t * LANES : (t + 1) * LANES]
        pairs[t, :, : tile.shape[1]] = tile
    for half in range(2):
        values = [pairs[t, pl.ds(half, WIDTH, stride=2), :] for t in range(tiles)]
        values = jnp.concatenate(values, axis=1)
        base = values[:, SPAN : SPAN + ROWS]
        values = values[:, :SPAN] + jnp.concatenate([base] * HALF, axis=1)
        mean = jnp.mean(values, axis=0, keepdims=True)
        centred = values - mean
        var = jnp.mean(centred * centred, axis=0, keepdims=True)
        onorm = (centred * lax.rsqrt(var + 1e-05) * gain_ref[...] + bias_ref[...]).astype(BF16)
        update = dot(onorm, w_ref[...], ((0,), (0,))) * gate_ref[half * SPAN : (half + 1) * SPAN]
        for j in range(HALF):
            tokens[pl.ds(half * HALF + j, ROWS, stride=COLS), :] = update[j * ROWS : (j + 1) * ROWS]
    out_ref[...] = tokens[...].astype(BF16)


def per_device(
    pair, pair_mask, in_gain, in_bias, proj_weight, gate_weight, out_gain, out_bias, out_weight
):
    shape = jax.ShapeDtypeStruct
    count = ROWS * COLS
    given = pair.reshape(count, WIDTH), pair_mask.T, in_gain[None], in_bias[None], proj_weight
    send, normed = pl.pallas_call(
        factors_kernel,
        out_shape=(shape((WIDTH, 2, 2 * SPAN), BF16), shape((count, WIDTH), BF16)),
        in_specs=[pl.BlockSpec(memory_space=pl.ANY)] * 5,
        scratch_shapes=[pltpu.VMEM(value.shape, value.dtype) for value in given]
        + [
            pltpu.VMEM((count, WIDTH), F32),
            pltpu.VMEM((2 * SPAN // LANES, 2 * WIDTH, LANES), F32),
            pltpu.SemaphoreType.DMA((5,)),
        ],
        compiler_params=pltpu.CompilerParams(vmem_limit_bytes=56 * 2**20),
        name="factors",
    )(*given)
    exchange = functools.partial(
        lax.all_to_all, axis_name=AXES, split_axis=0, concat_axis=0, axis_index_groups=channel_groups(), tiled=True
    )
    core = lax.rem(lax.axis_index("col"), 2).astype(jnp.int32).reshape(1)
    side = (lax.rem(lax.axis_index("row"), 4) // 2).astype(jnp.int32).reshape(1)
    vmem, smem = pl.BlockSpec(memory_space=pltpu.VMEM), pl.BlockSpec(memory_space=pltpu.SMEM)
    both = exchange(send)
    last = out_gain[:, None], out_bias[:, None], out_weight
    late = call(
        gate_kernel, [shape((count, WIDTH), F32)] + [shape(value.shape, value.dtype) for value in last], name="gate"
    )(normed, gate_weight, *last)
    keep, away = pl.pallas_call(
        right_kernel,
        out_shape=(shape((JSPAN, SIDE), BF16),) * 2,
        in_specs=[vmem, smem],
        compiler_params=pltpu.CompilerParams(vmem_limit_bytes=16 * 2**20),
        name="right",
    )(both, core)
    late, keep = lax.optimization_barrier((late, keep))
    mirror = lax.ppermute(keep, AXES, swap(True, False))
    cross = lax.ppermute(away, AXES, swap(True, True))
    bundle = call(left_kernel, shape((SIDE + JSPAN, SIDE), BF16), name="left")(both, away)
    bundle_core = lax.ppermute(bundle, AXES, swap(False, True))
    own = pl.pallas_call(
        own_kernel,
        out_shape=shape((SIDE // LANES, SIDE, LANES), F32),
        in_specs=[vmem] * 3 + [smem],
        compiler_params=pltpu.CompilerParams(vmem_limit_bytes=16 * 2**20),
        cost_estimate=pl.CostEstimate(flops=SIDE * SIDE * SIDE * 2 * COST_SCALE, bytes_accessed=0, transcendentals=0),
        name="own",
    )(bundle, keep, mirror, side)
    combined = pl.pallas_call(
        contract_kernel,
        out_shape=shape((RPOS * QPOS, 2, SPAN + ROWS), BF16),
        in_specs=[vmem] * 3 + [smem],
        scratch_shapes=[pltpu.VMEM((SIDE // LANES, SIDE, LANES), F32)],
        compiler_params=pltpu.CompilerParams(vmem_limit_bytes=16 * 2**20),
        name="contract",
    )(bundle_core, cross, own, side)
    combined = exchange(combined)
    update = call(
        update_kernel,
        shape((count, WIDTH), BF16),
        (pltpu.VMEM((pl.cdiv(SPAN + ROWS, LANES), 2 * WIDTH, LANES), F32), pltpu.VMEM((count, WIDTH), F32)),
        "update",
    )(combined, *late)
    return update.reshape(ROWS, COLS, WIDTH)


def solution(mesh):
    return jax.shard_map(
        per_device,
        mesh=mesh,
        in_specs=(P("row", "col", None), P("row", "col"), P(), P(), P(), P(), P(), P(), P()),
        out_specs=P("row", "col", None),
        check_vma=False,
    )
```

```python
import functools

import jax
import jax.numpy as jnp
from jax import lax
from jax.experimental import pallas as pl
from jax.experimental.pallas import tpu as pltpu
from jax.sharding import PartitionSpec as P

BF16 = jnp.bfloat16
F32 = jnp.float32
AXES = ("row", "col")
ROWS, COLS, WIDTH = 48, 24, 128
COST_SCALE = 100
HALF = COLS // 2
SPAN = HALF * ROWS
RPOS, QPOS = 8, 16
LANES = 128
SIDE = RPOS * ROWS
JSPAN = RPOS * COLS


def sigmoid(x):
    return 0.5 * jnp.tanh(0.5 * x) + 0.5


def device(z_hi, x, z_lo, y, core):
    return (z_hi * 4 + x) * 32 + z_lo * 16 + y * 2 + core


def x_of(side, x_low):
    return x_low if side == 0 else 3 - x_low


def ring(a, b):
    return min((a - b) % 8, (b - a) % 8)


def from_far(items, first, distance):
    return [first] + sorted([item for item in items if item != first], key=lambda item: -distance(item))


ROW_ORDER = from_far(
    [(zh, xl) for zh in range(4) for xl in range(2)], (2, 0), lambda place: (ring(2 * place[0], 5) + ring(2 * place[0] + 1, 5)) / 2 + place[1]
)
COL_ORDER = from_far(
    [(zl, y) for zl in range(2) for y in range(8)], (1, 4), lambda place: ring(place[1], 4) + (1 - place[0]) / 2
)


def positions():
    return [(zh, xl, zl, y) for zh, xl in ROW_ORDER for zl, y in COL_ORDER]


def column_position(z_hi, x):
    row = z_hi * 4 + x
    return COL_ORDER.index((row // 8, row % 8))


def channel_groups():
    return [
        [device(zh, x_of(side, xl), zl, y, core) for zh, xl, zl, y in positions()]
        for side in range(2)
        for core in range(2)
    ]


def swap(mirror, core):
    return [
        (device(zh, x, zl, y, c), device(zh, 3 - x if mirror else x, zl, y, 1 - c if core else c))
        for zh in range(4)
        for x in range(4)
        for zl in range(2)
        for y in range(8)
        for c in range(2)
    ]


def dot(a, b, dims):
    return lax.dot_general(a, b, (dims, ((), ())), preferred_element_type=F32)


def call(kernel, out_shape, scratch=(), name=None):
    return pl.pallas_call(
        kernel,
        out_shape=out_shape,
        scratch_shapes=list(scratch),
        compiler_params=pltpu.CompilerParams(vmem_limit_bytes=16 * 2**20),
        name=name,
    )


def factors_kernel(*refs):
    given, (send_ref, normed_ref), held = refs[:5], refs[5:7], refs[7:12]
    tokens, pairs, sems = refs[12:]
    copies = [pltpu.make_async_copy(src, dst, sems.at[n]) for n, (src, dst) in enumerate(zip(given, held))]
    for copy in copies:
        copy.start()
    for copy in copies:
        copy.wait()
    x_ref, mask_ref, gain_ref, bias_ref, w_ref = held
    tokens[...] = x_ref[...].astype(F32)
    values = jnp.concatenate([tokens[pl.ds(k, ROWS, stride=COLS), :] for k in range(COLS)], axis=0)
    mean = jnp.mean(values, axis=-1, keepdims=True)
    centred = values - mean
    var = jnp.mean(centred * centred, axis=-1, keepdims=True)
    normed = (centred * lax.rsqrt(var + 1e-05) * gain_ref[...] + bias_ref[...]).astype(BF16)
    normed_ref[...] = normed
    token = lax.broadcasted_iota(jnp.int32, (ROWS, ROWS * COLS), 1)
    spread = (lax.rem(token, ROWS) == lax.broadcasted_iota(jnp.int32, token.shape, 0)).astype(BF16)
    every = dot(mask_ref[...].astype(F32).astype(BF16), spread, ((1,), (0,)))
    token = lax.broadcasted_iota(jnp.int32, every.shape, 1)
    first = lax.broadcasted_iota(jnp.int32, every.shape, 0) * ROWS
    mask = jnp.sum(jnp.where((token >= first) & (token < first + ROWS), every, 0.0), axis=0, keepdims=True)
    weight = w_ref[...].T
    for half in range(2):
        part = normed[half * SPAN : (half + 1) * SPAN]
        part_mask = mask[:, half * SPAN : (half + 1) * SPAN]
        sides = []
        for side in range(2):
            hidden = dot(weight[side * 2 * WIDTH : (side + 1) * 2 * WIDTH], part, ((1,), (1,)))
            sides.append(sigmoid(hidden[WIDTH:]) * hidden[:WIDTH] * part_mask)
        both = jnp.concatenate(sides, axis=1)
        for t in range(2 * SPAN // LANES):
            pairs[t, pl.ds(half, WIDTH, stride=2), :] = both[:, t * LANES : (t + 1) * LANES]
    for t in range(2 * SPAN // LANES):
        send_ref[:, :, t * LANES : (t + 1) * LANES] = pairs[t].astype(BF16).reshape(WIDTH, 2, LANES)


def gate_kernel(normed_ref, w_ref, *rest_refs):
    *from_refs, gate_ref, gain_ref, bias_ref, out_w_ref = rest_refs
    gate_ref[...] = sigmoid(dot(normed_ref[...], w_ref[...], ((1,), (0,))))
    for source, target in zip(from_refs, (gain_ref, bias_ref, out_w_ref)):
        target[...] = source[...]


def right_kernel(x_ref, core_ref, keep_ref, send_ref):
    x = x_ref[...].reshape(RPOS * QPOS * 2, 2 * SPAN)[:, SPAN:]
    core = core_ref[0]
    rows = 2 * QPOS
    for k in range(HALF // 2):
        blocks = [
            jnp.concatenate(
                [
                    x[rp * rows : (rp + 1) * rows, (h * 6 + k) * ROWS + b * COLS : (h * 6 + k) * ROWS + (b + 1) * COLS]
                    for h in range(2)
                    for rp in range(RPOS)
                ],
                axis=1,
            )
            for b in range(2)
        ]
        keep_ref[k * rows : (k + 1) * rows, :] = jnp.where(core == 0, blocks[0], blocks[1])
        send_ref[k * rows : (k + 1) * rows, :] = jnp.where(core == 0, blocks[1], blocks[0])


def left_kernel(x_ref, away_ref, out_ref):
    x = x_ref[...].reshape(RPOS * QPOS * 2, 2 * SPAN)[:, :SPAN]
    rows = 2 * QPOS
    for k in range(HALF):
        out_ref[k * rows : (k + 1) * rows, :] = jnp.concatenate(
            [x[rp * rows : (rp + 1) * rows, k * ROWS : (k + 1) * ROWS] for rp in range(RPOS)], axis=1
        )
    out_ref[SIDE:, :] = away_ref[...]


def add_products(left, here, mirror, side, total, earlier=None):
    for at, right in ((side, here), (1 - side, mirror)):
        part = jnp.zeros((JSPAN, SIDE), F32)
        for h in range(2):
            part += dot(right[:, h * JSPAN : (h + 1) * JSPAN], left[h * JSPAN : (h + 1) * JSPAN], ((0,), (0,)))
        for rp, (z_hi, x_low) in enumerate(ROW_ORDER):
            places = [column_position(z_hi, x_of(s, x_low)) * COLS for s in range(2)]
            rows = pl.ds(pl.multiple_of(jnp.where(at == 0, places[0], places[1]), 8), COLS)
            for t in range(SIDE // LANES):
                piece = part[rp * COLS : (rp + 1) * COLS, t * LANES : (t + 1) * LANES]
                total[t, rows, :] = piece if earlier is None else piece + earlier[t, rows, :]


def own_kernel(bundle_ref, keep_ref, mirror_ref, side_ref, total_ref):
    add_products(bundle_ref[:SIDE], keep_ref[...], mirror_ref[...], side_ref[0], total_ref)


def contract_kernel(bundle_ref, cross_ref, own_ref, side_ref, send_ref, total):
    add_products(bundle_ref[:SIDE], bundle_ref[SIDE:], cross_ref[...], side_ref[0], total, own_ref)
    rows = 2 * QPOS
    blocks = [
        jnp.concatenate([total[t, pl.ds(j, rows, stride=HALF), :] for t in range(SIDE // LANES)], axis=1)
        for j in range(HALF)
    ]
    base = (functools.reduce(jnp.add, blocks) * (1.0 / HALF)).astype(BF16).astype(F32)
    blocks = [block - base for block in blocks] + [base]
    for rp in range(RPOS):
        piece = jnp.concatenate([block[:, rp * ROWS : (rp + 1) * ROWS] for block in blocks], axis=1)
        send_ref[rp * QPOS : (rp + 1) * QPOS] = piece.astype(BF16).reshape(QPOS, 2, SPAN + ROWS)


def update_kernel(x_ref, gate_ref, gain_ref, bias_ref, w_ref, out_ref, pairs, tokens):
    arrived = x_ref[...].reshape(2 * WIDTH, SPAN + ROWS).astype(F32)
    tiles = pl.cdiv(SPAN + ROWS, LANES)
    for t in range(tiles):
        tile = arrived[:, t * LANES : (t + 1) * LANES]
        pairs[t, :, : tile.shape[1]] = tile
    for half in range(2):
        values = [pairs[t, pl.ds(half, WIDTH, stride=2), :] for t in range(tiles)]
        values = jnp.concatenate(values, axis=1)
        base = values[:, SPAN : SPAN + ROWS]
        values = values[:, :SPAN] + jnp.concatenate([base] * HALF, axis=1)
        mean = jnp.mean(values, axis=0, keepdims=True)
        centred = values - mean
        var = jnp.mean(centred * centred, axis=0, keepdims=True)
        onorm = (centred * lax.rsqrt(var + 1e-05) * gain_ref[...] + bias_ref[...]).astype(BF16)
        update = dot(onorm, w_ref[...], ((0,), (0,))) * gate_ref[half * SPAN : (half + 1) * SPAN]
        for j in range(HALF):
            tokens[pl.ds(half * HALF + j, ROWS, stride=COLS), :] = update[j * ROWS : (j + 1) * ROWS]
    out_ref[...] = tokens[...].astype(BF16)


def per_device(
    pair, pair_mask, in_gain, in_bias, proj_weight, gate_weight, out_gain, out_bias, out_weight
):
    shape = jax.ShapeDtypeStruct
    count = ROWS * COLS
    given = pair.reshape(count, WIDTH), pair_mask.T, in_gain[None], in_bias[None], proj_weight
    send, normed = pl.pallas_call(
        factors_kernel,
        out_shape=(shape((WIDTH, 2, 2 * SPAN), BF16), shape((count, WIDTH), BF16)),
        in_specs=[pl.BlockSpec(memory_space=pl.ANY)] * 5,
        scratch_shapes=[pltpu.VMEM(value.shape, value.dtype) for value in given]
        + [
            pltpu.VMEM((count, WIDTH), F32),
            pltpu.VMEM((2 * SPAN // LANES, 2 * WIDTH, LANES), F32),
            pltpu.SemaphoreType.DMA((5,)),
        ],
        compiler_params=pltpu.CompilerParams(vmem_limit_bytes=56 * 2**20),
        name="factors",
    )(*given)
    exchange = functools.partial(
        lax.all_to_all, axis_name=AXES, split_axis=0, concat_axis=0, axis_index_groups=channel_groups(), tiled=True
    )
    core = lax.rem(lax.axis_index("col"), 2).astype(jnp.int32).reshape(1)
    side = (lax.rem(lax.axis_index("row"), 4) // 2).astype(jnp.int32).reshape(1)
    vmem, smem = pl.BlockSpec(memory_space=pltpu.VMEM), pl.BlockSpec(memory_space=pltpu.SMEM)
    both = exchange(send)
    last = out_gain[:, None], out_bias[:, None], out_weight
    late = call(
        gate_kernel, [shape((count, WIDTH), F32)] + [shape(value.shape, value.dtype) for value in last], name="gate"
    )(normed, gate_weight, *last)
    keep, away = pl.pallas_call(
        right_kernel,
        out_shape=(shape((JSPAN, SIDE), BF16),) * 2,
        in_specs=[vmem, smem],
        compiler_params=pltpu.CompilerParams(vmem_limit_bytes=16 * 2**20),
        name="right",
    )(both, core)
    late, keep = lax.optimization_barrier((late, keep))
    mirror = lax.ppermute(keep, AXES, swap(True, False))
    cross = lax.ppermute(away, AXES, swap(True, True))
    bundle = call(left_kernel, shape((SIDE + JSPAN, SIDE), BF16), name="left")(both, away)
    bundle_core = lax.ppermute(bundle, AXES, swap(False, True))
    own = pl.pallas_call(
        own_kernel,
        out_shape=shape((SIDE // LANES, SIDE, LANES), F32),
        in_specs=[vmem] * 3 + [smem],
        compiler_params=pltpu.CompilerParams(vmem_limit_bytes=16 * 2**20),
        cost_estimate=pl.CostEstimate(flops=SIDE * SIDE * SIDE * 2 * COST_SCALE, bytes_accessed=0, transcendentals=0),
        name="own",
    )(bundle, keep, mirror, side)
    combined = pl.pallas_call(
        contract_kernel,
        out_shape=shape((RPOS * QPOS, 2, SPAN + ROWS), BF16),
        in_specs=[vmem] * 3 + [smem],
        scratch_shapes=[pltpu.VMEM((SIDE // LANES, SIDE, LANES), F32)],
        compiler_params=pltpu.CompilerParams(vmem_limit_bytes=16 * 2**20),
        name="contract",
    )(bundle_core, cross, own, side)
    combined = exchange(combined)
    update = call(
        update_kernel,
        shape((count, WIDTH), BF16),
        (pltpu.VMEM((pl.cdiv(SPAN + ROWS, LANES), 2 * WIDTH, LANES), F32), pltpu.VMEM((count, WIDTH), F32)),
        "update",
    )(combined, *late)
    return update.reshape(ROWS, COLS, WIDTH)


def solution(mesh):
    return jax.shard_map(
        per_device,
        mesh=mesh,
        in_specs=(P("row", "col", None), P("row", "col"), P(), P(), P(), P(), P(), P(), P()),
        out_specs=P("row", "col", None),
        check_vma=False,
    )
```

```python
import functools

import jax
import jax.numpy as jnp
from jax import lax
from jax.experimental import pallas as pl
from jax.experimental.pallas import tpu as pltpu
from jax.sharding import PartitionSpec as P

BF16 = jnp.bfloat16
F32 = jnp.float32
AXES = ("row", "col")
ROWS, COLS, WIDTH = 48, 24, 128
COST_SCALE = 100
HALF = COLS // 2
SPAN = HALF * ROWS
RPOS, QPOS = 8, 16
LANES = 128
SIDE = RPOS * ROWS
JSPAN = RPOS * COLS


def sigmoid(x):
    return 0.5 * jnp.tanh(0.5 * x) + 0.5


def device(z_hi, x, z_lo, y, core):
    return (z_hi * 4 + x) * 32 + z_lo * 16 + y * 2 + core


def x_of(side, x_low):
    return x_low if side == 0 else 3 - x_low


def ring(a, b):
    return min((a - b) % 8, (b - a) % 8)


def from_far(items, first, distance):
    return [first] + sorted([item for item in items if item != first], key=lambda item: -distance(item))


ROW_ORDER = from_far(
    [(zh, xl) for zh in range(4) for xl in range(2)], (2, 0), lambda place: (ring(2 * place[0], 5) + ring(2 * place[0] + 1, 5)) / 2 - place[1] / 4
)
COL_ORDER = from_far(
    [(zl, y) for zl in range(2) for y in range(8)], (1, 4), lambda place: ring(place[1], 4) + (1 - place[0]) / 2
)


def positions():
    return [(zh, xl, zl, y) for zh, xl in ROW_ORDER for zl, y in COL_ORDER]


def column_position(z_hi, x):
    row = z_hi * 4 + x
    return COL_ORDER.index((row // 8, row % 8))


def channel_groups():
    return [
        [device(zh, x_of(side, xl), zl, y, core) for zh, xl, zl, y in positions()]
        for side in range(2)
        for core in range(2)
    ]


def swap(mirror, core):
    return [
        (device(zh, x, zl, y, c), device(zh, 3 - x if mirror else x, zl, y, 1 - c if core else c))
        for zh in range(4)
        for x in range(4)
        for zl in range(2)
        for y in range(8)
        for c in range(2)
    ]


def dot(a, b, dims):
    return lax.dot_general(a, b, (dims, ((), ())), preferred_element_type=F32)


def call(kernel, out_shape, scratch=(), name=None):
    return pl.pallas_call(
        kernel,
        out_shape=out_shape,
        scratch_shapes=list(scratch),
        compiler_params=pltpu.CompilerParams(vmem_limit_bytes=16 * 2**20),
        name=name,
    )


def factors_kernel(*refs):
    given, (send_ref, normed_ref), held = refs[:5], refs[5:7], refs[7:12]
    tokens, pairs, sems = refs[12:]
    copies = [pltpu.make_async_copy(src, dst, sems.at[n]) for n, (src, dst) in enumerate(zip(given, held))]
    for copy in copies:
        copy.start()
    for copy in copies:
        copy.wait()
    x_ref, mask_ref, gain_ref, bias_ref, w_ref = held
    tokens[...] = x_ref[...].astype(F32)
    values = jnp.concatenate([tokens[pl.ds(k, ROWS, stride=COLS), :] for k in range(COLS)], axis=0)
    mean = jnp.mean(values, axis=-1, keepdims=True)
    centred = values - mean
    var = jnp.mean(centred * centred, axis=-1, keepdims=True)
    normed = (centred * lax.rsqrt(var + 1e-05) * gain_ref[...] + bias_ref[...]).astype(BF16)
    normed_ref[...] = normed
    token = lax.broadcasted_iota(jnp.int32, (ROWS, ROWS * COLS), 1)
    spread = (lax.rem(token, ROWS) == lax.broadcasted_iota(jnp.int32, token.shape, 0)).astype(BF16)
    every = dot(mask_ref[...].astype(F32).astype(BF16), spread, ((1,), (0,)))
    token = lax.broadcasted_iota(jnp.int32, every.shape, 1)
    first = lax.broadcasted_iota(jnp.int32, every.shape, 0) * ROWS
    mask = jnp.sum(jnp.where((token >= first) & (token < first + ROWS), every, 0.0), axis=0, keepdims=True)
    weight = w_ref[...].T
    for half in range(2):
        part = normed[half * SPAN : (half + 1) * SPAN]
        part_mask = mask[:, half * SPAN : (half + 1) * SPAN]
        sides = []
        for side in range(2):
            hidden = dot(weight[side * 2 * WIDTH : (side + 1) * 2 * WIDTH], part, ((1,), (1,)))
            sides.append(sigmoid(hidden[WIDTH:]) * hidden[:WIDTH] * part_mask)
        both = jnp.concatenate(sides, axis=1)
        for t in range(2 * SPAN // LANES):
            pairs[t, pl.ds(half, WIDTH, stride=2), :] = both[:, t * LANES : (t + 1) * LANES]
    for t in range(2 * SPAN // LANES):
        send_ref[:, :, t * LANES : (t + 1) * LANES] = pairs[t].astype(BF16).reshape(WIDTH, 2, LANES)


def gate_kernel(normed_ref, w_ref, *rest_refs):
    *from_refs, gate_ref, gain_ref, bias_ref, out_w_ref = rest_refs
    gate_ref[...] = sigmoid(dot(normed_ref[...], w_ref[...], ((1,), (0,))))
    for source, target in zip(from_refs, (gain_ref, bias_ref, out_w_ref)):
        target[...] = source[...]


def right_kernel(x_ref, core_ref, keep_ref, send_ref):
    x = x_ref[...].reshape(RPOS * QPOS * 2, 2 * SPAN)[:, SPAN:]
    core = core_ref[0]
    rows = 2 * QPOS
    for k in range(HALF // 2):
        blocks = [
            jnp.concatenate(
                [
                    x[rp * rows : (rp + 1) * rows, (h * 6 + k) * ROWS + b * COLS : (h * 6 + k) * ROWS + (b + 1) * COLS]
                    for h in range(2)
                    for rp in range(RPOS)
                ],
                axis=1,
            )
            for b in range(2)
        ]
        keep_ref[k * rows : (k + 1) * rows, :] = jnp.where(core == 0, blocks[0], blocks[1])
        send_ref[k * rows : (k + 1) * rows, :] = jnp.where(core == 0, blocks[1], blocks[0])


def left_kernel(x_ref, away_ref, out_ref):
    x = x_ref[...].reshape(RPOS * QPOS * 2, 2 * SPAN)[:, :SPAN]
    rows = 2 * QPOS
    for k in range(HALF):
        out_ref[k * rows : (k + 1) * rows, :] = jnp.concatenate(
            [x[rp * rows : (rp + 1) * rows, k * ROWS : (k + 1) * ROWS] for rp in range(RPOS)], axis=1
        )
    out_ref[SIDE:, :] = away_ref[...]


def add_products(left, here, mirror, side, total, earlier=None):
    for at, right in ((side, here), (1 - side, mirror)):
        part = jnp.zeros((JSPAN, SIDE), F32)
        for h in range(2):
            part += dot(right[:, h * JSPAN : (h + 1) * JSPAN], left[h * JSPAN : (h + 1) * JSPAN], ((0,), (0,)))
        for rp, (z_hi, x_low) in enumerate(ROW_ORDER):
            places = [column_position(z_hi, x_of(s, x_low)) * COLS for s in range(2)]
            rows = pl.ds(pl.multiple_of(jnp.where(at == 0, places[0], places[1]), 8), COLS)
            for t in range(SIDE // LANES):
                piece = part[rp * COLS : (rp + 1) * COLS, t * LANES : (t + 1) * LANES]
                total[t, rows, :] = piece if earlier is None else piece + earlier[t, rows, :]


def own_kernel(bundle_ref, keep_ref, mirror_ref, side_ref, total_ref):
    add_products(bundle_ref[:SIDE], keep_ref[...], mirror_ref[...], side_ref[0], total_ref)


def contract_kernel(bundle_ref, cross_ref, own_ref, side_ref, send_ref, total):
    add_products(bundle_ref[:SIDE], bundle_ref[SIDE:], cross_ref[...], side_ref[0], total, own_ref)
    rows = 2 * QPOS
    blocks = [
        jnp.concatenate([total[t, pl.ds(j, rows, stride=HALF), :] for t in range(SIDE // LANES)], axis=1)
        for j in range(HALF)
    ]
    base = (functools.reduce(jnp.add, blocks) * (1.0 / HALF)).astype(BF16).astype(F32)
    blocks = [block - base for block in blocks] + [base]
    for rp in range(RPOS):
        piece = jnp.concatenate([block[:, rp * ROWS : (rp + 1) * ROWS] for block in blocks], axis=1)
        send_ref[rp * QPOS : (rp + 1) * QPOS] = piece.astype(BF16).reshape(QPOS, 2, SPAN + ROWS)


def update_kernel(x_ref, gate_ref, gain_ref, bias_ref, w_ref, out_ref, pairs, tokens):
    arrived = x_ref[...].reshape(2 * WIDTH, SPAN + ROWS).astype(F32)
    tiles = pl.cdiv(SPAN + ROWS, LANES)
    for t in range(tiles):
        tile = arrived[:, t * LANES : (t + 1) * LANES]
        pairs[t, :, : tile.shape[1]] = tile
    for half in range(2):
        values = [pairs[t, pl.ds(half, WIDTH, stride=2), :] for t in range(tiles)]
        values = jnp.concatenate(values, axis=1)
        base = values[:, SPAN : SPAN + ROWS]
        values = values[:, :SPAN] + jnp.concatenate([base] * HALF, axis=1)
        mean = jnp.mean(values, axis=0, keepdims=True)
        centred = values - mean
        var = jnp.mean(centred * centred, axis=0, keepdims=True)
        onorm = (centred * lax.rsqrt(var + 1e-05) * gain_ref[...] + bias_ref[...]).astype(BF16)
        update = dot(onorm, w_ref[...], ((0,), (0,))) * gate_ref[half * SPAN : (half + 1) * SPAN]
        for j in range(HALF):
            tokens[pl.ds(half * HALF + j, ROWS, stride=COLS), :] = update[j * ROWS : (j + 1) * ROWS]
    out_ref[...] = tokens[...].astype(BF16)


def per_device(
    pair, pair_mask, in_gain, in_bias, proj_weight, gate_weight, out_gain, out_bias, out_weight
):
    shape = jax.ShapeDtypeStruct
    count = ROWS * COLS
    given = pair.reshape(count, WIDTH), pair_mask.T, in_gain[None], in_bias[None], proj_weight
    send, normed = pl.pallas_call(
        factors_kernel,
        out_shape=(shape((WIDTH, 2, 2 * SPAN), BF16), shape((count, WIDTH), BF16)),
        in_specs=[pl.BlockSpec(memory_space=pl.ANY)] * 5,
        scratch_shapes=[pltpu.VMEM(value.shape, value.dtype) for value in given]
        + [
            pltpu.VMEM((count, WIDTH), F32),
            pltpu.VMEM((2 * SPAN // LANES, 2 * WIDTH, LANES), F32),
            pltpu.SemaphoreType.DMA((5,)),
        ],
        compiler_params=pltpu.CompilerParams(vmem_limit_bytes=56 * 2**20),
        name="factors",
    )(*given)
    exchange = functools.partial(
        lax.all_to_all, axis_name=AXES, split_axis=0, concat_axis=0, axis_index_groups=channel_groups(), tiled=True
    )
    core = lax.rem(lax.axis_index("col"), 2).astype(jnp.int32).reshape(1)
    side = (lax.rem(lax.axis_index("row"), 4) // 2).astype(jnp.int32).reshape(1)
    vmem, smem = pl.BlockSpec(memory_space=pltpu.VMEM), pl.BlockSpec(memory_space=pltpu.SMEM)
    both = exchange(send)
    last = out_gain[:, None], out_bias[:, None], out_weight
    late = call(
        gate_kernel, [shape((count, WIDTH), F32)] + [shape(value.shape, value.dtype) for value in last], name="gate"
    )(normed, gate_weight, *last)
    keep, away = pl.pallas_call(
        right_kernel,
        out_shape=(shape((JSPAN, SIDE), BF16),) * 2,
        in_specs=[vmem, smem],
        compiler_params=pltpu.CompilerParams(vmem_limit_bytes=16 * 2**20),
        name="right",
    )(both, core)
    late, keep = lax.optimization_barrier((late, keep))
    mirror = lax.ppermute(keep, AXES, swap(True, False))
    cross = lax.ppermute(away, AXES, swap(True, True))
    bundle = call(left_kernel, shape((SIDE + JSPAN, SIDE), BF16), name="left")(both, away)
    bundle_core = lax.ppermute(bundle, AXES, swap(False, True))
    own = pl.pallas_call(
        own_kernel,
        out_shape=shape((SIDE // LANES, SIDE, LANES), F32),
        in_specs=[vmem] * 3 + [smem],
        compiler_params=pltpu.CompilerParams(vmem_limit_bytes=16 * 2**20),
        cost_estimate=pl.CostEstimate(flops=SIDE * SIDE * SIDE * 2 * COST_SCALE, bytes_accessed=0, transcendentals=0),
        name="own",
    )(bundle, keep, mirror, side)
    combined = pl.pallas_call(
        contract_kernel,
        out_shape=shape((RPOS * QPOS, 2, SPAN + ROWS), BF16),
        in_specs=[vmem] * 3 + [smem],
        scratch_shapes=[pltpu.VMEM((SIDE // LANES, SIDE, LANES), F32)],
        compiler_params=pltpu.CompilerParams(vmem_limit_bytes=16 * 2**20),
        name="contract",
    )(bundle_core, cross, own, side)
    combined = exchange(combined)
    update = call(
        update_kernel,
        shape((count, WIDTH), BF16),
        (pltpu.VMEM((pl.cdiv(SPAN + ROWS, LANES), 2 * WIDTH, LANES), F32), pltpu.VMEM((count, WIDTH), F32)),
        "update",
    )(combined, *late)
    return update.reshape(ROWS, COLS, WIDTH)


def solution(mesh):
    return jax.shard_map(
        per_device,
        mesh=mesh,
        in_specs=(P("row", "col", None), P("row", "col"), P(), P(), P(), P(), P(), P(), P()),
        out_specs=P("row", "col", None),
        check_vma=False,
    )
```
